32 devices in a mesh: dp: 4 (over y, core), tensor: 8 (over z, x).
Axes of the slice: x: 2, y: 2, z: 4, core: 2. Of those that a mesh axis runs over, the one named last changes fastest.
Arguments:
- tokens: bfloat16 [2048, 2048], P(('dp', 'tensor')), may hold values from -6 to 6
- norm_gain: bfloat16 [2048], replicated, may hold values from 0.25 to 1.75
- query_weight: bfloat16 [2048, 2048], P('dp'), may hold values from -0.125 to 0.125
- keyval_weight: bfloat16 [2, 2048, 512], P(None, 'dp'), may hold values from -0.125 to 0.125
- query_gain: float32 [64], replicated, may hold values from 0.5 to 2
- key_gain: float32 [64], replicated, may hold values from 0.5 to 2
- output_weight: bfloat16 [2048, 2048], P(None, 'dp'), may hold values from -0.75 to 0.75
- keyval_cache: bfloat16 [32, 2048, 128], P(('dp', 'tensor')), may hold values from -96 to 96
- cached_lengths: int32 [4], P('dp'), may hold values from 1 to 2048, as said below
- sink_count: int32 [4], P('dp'), may hold values from 1 to 32
- window: int32 [4], P('dp'), may hold values from 512 to 4096, as said below
Outputs:
- attended: bfloat16 [2048, 2048], P(('dp', 'tensor'))
- fresh_keyvals: bfloat16 [32, 512, 128], P(('dp', 'tensor'))
The draws below stay inside these ranges and needn't reach their ends.
Inputs may be any that keep to these rules, and one draw needn't show every extreme that they name: `cached_lengths`: some request has exactly 2048 cached tokens. Some request has a window of exactly 4096.
All inputs are finite; a program needn't handle non-finite values.
Results may differ from the reference program's by a relative error of at most 0.014.
The reference program's roundings to bfloat16 on the way count: a program that leaves them out, or rounds other values in their place, can miss the bound.
Values may be sent and summed in bfloat16 or wider, within the bound.
No kernel may reach another device: no remote copies, remote signals or barrier semaphores. Data moves between devices by JAX's collectives and lax.ppermute only.
A program may use at most 64 MiB of HBM per device.

```python
import math
import jax
import jax.numpy as jnp
from jax import lax

D = 2048
HEADS = 32
KVH = 8
HD = 64
NEW = 512
CACHE = 2048
WINDOW = 4096
REQS = 4


def draw_cached_lengths(key, part):
    first_key, second_key = jax.random.split(jax.random.fold_in(key, 11))
    lengths = jax.random.randint(first_key, (REQS,), 1, CACHE + 1)
    chosen = jax.random.randint(second_key, (), 0, REQS)
    return jnp.where(jnp.arange(REQS) == chosen, CACHE, lengths).astype(jnp.int32)


def draw_window(key, part):
    first_key, second_key = jax.random.split(jax.random.fold_in(key, 23))
    widths = jax.random.randint(first_key, (REQS,), WINDOW // 8, WINDOW + 1)
    chosen = jax.random.randint(second_key, (), 0, REQS)
    return jnp.where(jnp.arange(REQS) == chosen, WINDOW, widths).astype(jnp.int32)


def draw_keyval_cache(key, part):
    parts_keys = jax.random.split(jax.random.fold_in(key, 37), 6)
    shape = (REQS * KVH, CACHE, 2 * HD)
    return jnp.clip(jax.random.normal(parts_keys[5], shape, jnp.float32), -6.0, 6.0).astype(jnp.bfloat16)


def plant(drawn, stream_key, low, high):
    longest = drawn.shape.index(max(drawn.shape))
    spots = []
    for shift in (0, 1):
        where = [jax.random.randint(jax.random.fold_in(stream_key, axis), (), 0, length) for axis, length in enumerate(drawn.shape)]
        where[longest] = (where[longest] + shift) % drawn.shape[longest]
        spots.append(tuple(where))
    return drawn.at[spots[0]].set(low).at[spots[1]].set(high)


def level_of(rng, extent, shards, least, largest):
    level = 1.0
    for position, shards_of in shards:
        draws = jax.random.uniform(jax.random.fold_in(jax.random.fold_in(rng, 6), position), (shards_of,), jnp.float32, least / len(shards), largest / len(shards))
        level = level * jnp.repeat(jnp.exp(draws), extent[position] // shards_of).reshape((-1,) + (1,) * (len(extent) - 1 - position))
    return level


def gaussian(own_key, extent, deviation, reach, cuts=(), kind=jnp.bfloat16):
    factor_of = level_of(own_key, extent, cuts, -0.22, 0.18) if cuts else 1.0
    drawn = jax.random.normal(own_key, extent, jnp.float32) * deviation * factor_of
    return jnp.minimum(jnp.maximum(drawn, -reach), reach).astype(kind)


def setup_inputs(seed: int = 0) -> dict:
    splits = jax.random.split(jax.random.key(seed), 12)
    tokens = gaussian(splits[0], (REQS * NEW, D), 1.0, 6.0, ((0, 32),))
    norm_gain = jnp.clip(1.0 + 0.15 * jax.random.normal(splits[1], (D,), jnp.float32), 0.25, 1.75).astype(jnp.bfloat16)
    query_weight = gaussian(splits[2], (D, HEADS * HD), D ** -0.5, 0.125, ((0, 4),))
    keyval_weight = gaussian(splits[3], (2, D, KVH * HD), D ** -0.5, 0.125, ((1, 4),))
    query_gain = jnp.clip(jnp.exp(jax.random.uniform(splits[4], (HD,), jnp.float32, math.log(0.5), math.log(2.0))), 0.5, 2.0)
    key_gain = jnp.clip(jnp.exp(jax.random.uniform(splits[5], (HD,), jnp.float32, math.log(0.5), math.log(2.0))), 0.5, 2.0)
    output_weight = gaussian(splits[6], (HEADS * HD, D), HD ** -0.5, 0.75, ((1, 4),))
    keyval_cache = draw_keyval_cache(jax.random.fold_in(splits[11], 71), 0)
    cached_lengths = draw_cached_lengths(jax.random.fold_in(splits[11], 71), 0)
    sink_count = plant(jax.random.randint(splits[9], (REQS,), 1, 33), jax.random.fold_in(splits[9], 1), 1, 32).astype(jnp.int32)
    window = draw_window(jax.random.fold_in(splits[11], 71), 0)
    return {"tokens": tokens, "norm_gain": norm_gain, "query_weight": query_weight, "keyval_weight": keyval_weight, "query_gain": query_gain, "key_gain": key_gain, "output_weight": output_weight, "keyval_cache": keyval_cache, "cached_lengths": cached_lengths, "sink_count": sink_count, "window": window}


epsilon = 1e-05
theta_base = 1000000.0

def rms_scale(values, weights):
    mean_square = lax.optimization_barrier(jnp.mean(values * values, axis=-1, keepdims=True))
    return values * lax.rsqrt(mean_square + epsilon) * weights

def rotate(values, positions):
    half_dim = values.shape[-1] // 2
    inverse_freq = theta_base ** (-2.0 * jnp.arange(half_dim, dtype=jnp.float32) / values.shape[-1])
    angles = positions.astype(jnp.float32)[:, None] * inverse_freq[None, :]
    cosine = jnp.cos(angles)
    sine_part = jnp.sin(angles)
    first_half = values[..., :half_dim]
    second_half = values[..., half_dim:]
    return jnp.concatenate([first_half * cosine - second_half * sine_part, second_half * cosine + first_half * sine_part], axis=-1)

def reference(tokens, norm_gain, query_weight, keyval_weight, query_gain, key_gain, output_weight, keyval_cache, cached_lengths, sink_count, window):
    group_size = HEADS // KVH
    scale = HD ** (-0.5)
    request_tokens_all = tokens.reshape(REQS, NEW, D)
    caches = keyval_cache.reshape(REQS, KVH, CACHE, 2 * HD)

    def one_request(operands):
        request_tokens, request_cache, length, sink_total, window_len = operands
        normed = rms_scale(request_tokens.astype(jnp.float32), norm_gain.astype(jnp.float32)).astype(jnp.bfloat16)
        query_raw = jnp.dot(normed, query_weight, preferred_element_type=jnp.float32).reshape(NEW, HEADS, HD).transpose(1, 0, 2)
        key_raw = jnp.dot(normed, keyval_weight[0], preferred_element_type=jnp.float32).reshape(NEW, KVH, HD).transpose(1, 0, 2)
        value_new = jnp.dot(normed, keyval_weight[1], preferred_element_type=jnp.float32).astype(jnp.bfloat16).reshape(NEW, KVH, HD).transpose(1, 0, 2)
        positions = length + jnp.arange(NEW, dtype=jnp.int32)
        queries = rotate(rms_scale(query_raw, query_gain), positions).astype(jnp.bfloat16)
        key_new = rotate(rms_scale(key_raw, key_gain), positions).astype(jnp.bfloat16)
        fresh_rows = jnp.concatenate([key_new, value_new], axis=2)
        all_keys = jnp.concatenate([request_cache[:, :, :HD], key_new], axis=1)
        all_values = jnp.concatenate([request_cache[:, :, HD:], value_new], axis=1)
        cache_slots = jnp.arange(CACHE, dtype=jnp.int32)
        key_pos = jnp.concatenate([cache_slots, positions])
        key_live = jnp.concatenate([cache_slots < length, jnp.ones((NEW,), jnp.bool_)])
        allowed = key_live[None, :] & (key_pos[None, :] <= positions[:, None]) & ((key_pos[None, :] < sink_total) | (positions[:, None] - key_pos[None, :] < window_len))

        def one_head(head_index):
            keys_here = all_keys[head_index // group_size].astype(jnp.float32)
            values_here = all_values[head_index // group_size].astype(jnp.float32)
            scores = jnp.dot(queries[head_index].astype(jnp.float32), keys_here.T) * scale
            row_max = lax.optimization_barrier(jnp.max(jnp.where(allowed, scores, -jnp.inf), axis=1, keepdims=True))
            weights = jnp.where(allowed, jnp.exp(scores - row_max), 0.0)
            total = lax.optimization_barrier(jnp.sum(weights, axis=1, keepdims=True))
            mixed = jnp.dot(weights.astype(jnp.bfloat16).astype(jnp.float32), values_here)
            return (mixed / total).astype(jnp.bfloat16)
        head_outputs = lax.map(one_head, jnp.arange(HEADS, dtype=jnp.int32))
        joined = head_outputs.transpose(1, 0, 2).reshape(NEW, HEADS * HD)
        attended_rows = jnp.dot(joined, output_weight, preferred_element_type=jnp.float32).astype(jnp.bfloat16)
        return (attended_rows, fresh_rows)
    attended, fresh_keyvals = lax.map(one_request, (request_tokens_all, caches, cached_lengths, sink_count, window))
    return (attended.reshape(REQS * NEW, D), fresh_keyvals.reshape(REQS * KVH, NEW, 2 * HD))
```

```python
import functools

import jax
import jax.numpy as jnp
from jax import lax
from jax.experimental import pallas as pl
from jax.experimental.pallas import tpu as pltpu
from jax.sharding import PartitionSpec as P

epsilon = 1e-05
theta_base = 1000000.0
masked_score = -1e30
vmem_bytes = 48 * 1024 * 1024


def rope_tables(positions, head_dim):
    half_dim = head_dim // 2
    inverse_freq = theta_base ** (-2.0 * jnp.arange(half_dim, dtype=jnp.float32) / head_dim)
    angles = positions.astype(jnp.float32)[:, None] * inverse_freq[None, :]
    cosine = jnp.cos(angles)
    sine = jnp.sin(angles)
    return (
        jnp.concatenate([cosine] * 4, axis=1),
        jnp.concatenate([-sine, sine] * 2, axis=1),
    )


def lanes_of(value):
    return lax.broadcasted_iota(jnp.int32, value.shape, value.ndim - 1)


def norm_rope_pair(pair, gain, cosine, sine, head_dim):
    lane = lanes_of(pair)
    low = lane < head_dim
    squared = pair * pair
    low_sum = jnp.sum(jnp.where(low, squared, 0.0), axis=1, keepdims=True)
    high_sum = jnp.sum(jnp.where(low, 0.0, squared), axis=1, keepdims=True)
    inverse = jnp.where(
        low,
        lax.rsqrt(low_sum / head_dim + epsilon),
        lax.rsqrt(high_sum / head_dim + epsilon),
    )
    normed = pair * inverse * gain
    half_dim = head_dim // 2
    swapped = jnp.where(
        lane % head_dim < half_dim,
        pltpu.roll(normed, 2 * head_dim - half_dim, 1),
        pltpu.roll(normed, half_dim, 1),
    )
    return normed * cosine + swapped * sine


def table_entry(table, index):
    found = jnp.int32(table[0])
    for place in range(1, len(table)):
        found = jnp.where(index == place, jnp.int32(table[place]), found)
    return found


def stage_kernel(plan, final, length_ref, window_ref, *refs):
    old, offsets, parts = plan["old"], plan["offsets"], plan["parts"]
    pieces, head_dim, ring = plan["pieces"], plan["head_dim"], plan["ring"]
    new = sum(parts_of_block for parts_of_block in parts)
    refs = list(refs)

    def take(count):
        taken = refs[:count]
        del refs[:count]
        return taken

    tokens = take(new)
    norm_gain, query_gain, key_gain, cosine_ref, sine_ref, keys_ref, values_ref, reach_ref = take(8)
    weights = take(pieces)
    if old:
        queries_in, keyval_in, stats_in = take(3)
    if final:
        heads_out, fresh_out = take(2)
    else:
        queries_out, keyval_out, stats_out = take(3)
    normed_ref, projected_ref = take(2)
    if final:
        queries_out, keyval_out, stats_out = take(3)
    new_keys_ref, new_values_ref = take(2)

    fresh_blocks = len(parts)
    blocks = old + fresh_blocks
    members = len(ring)
    rows = normed_ref.shape[0] // fresh_blocks
    lanes = 2 * head_dim
    query_cols = projected_ref.shape[1] - lanes
    pairs = query_cols // lanes
    count = 2 * pairs * rows
    length = length_ref[0]
    window_len = window_ref[0]
    rank = lax.axis_index("tensor")
    own = lax.axis_index("dp")
    if length_ref.shape[0] > 1:
        length = length_ref[rank // members]
        window_len = window_ref[rank // members]
    place = table_entry([ring.index(one) for one in range(members)], rank % members)
    ids = [table_entry(ring, (place + offset + members) % members) for offset in offsets]

    gain = norm_gain[...].astype(jnp.float32)
    start = 0
    for part in tokens:
        values = part[...].astype(jnp.float32)
        mean_square = jnp.mean(values * values, axis=1, keepdims=True)
        normed_ref[pl.ds(start, part.shape[0]), :] = (
            values * lax.rsqrt(mean_square + epsilon) * gain
        ).astype(jnp.bfloat16)
        start += part.shape[0]
    depth = weights[0].shape[0]
    total = None
    for piece in range(pieces):
        from_column = pl.multiple_of((own ^ piece) * depth, depth)
        term = jnp.dot(
            normed_ref[:, pl.ds(from_column, depth)],
            weights[piece][...],
            preferred_element_type=jnp.float32,
        )
        total = term if total is None else total + term
    projected_ref[...] = total
    scale = head_dim ** (-0.5)

    if old:
        queries_out[pl.ds(0, old * count), :] = queries_in[...]
        keyval_out[pl.ds(0, old * rows), :] = keyval_in[...]
    query_gains = jnp.concatenate([query_gain[...]] * 2, axis=1)
    key_gains = jnp.concatenate([key_gain[...]] * 2, axis=1)
    for block in range(fresh_blocks):
        from_row = pl.multiple_of(ids[old + block] * rows, rows)
        cosine = cosine_ref[pl.ds(from_row, rows), :]
        sine = sine_ref[pl.ds(from_row, rows), :]
        here = pl.ds(block * rows, rows)
        for pair in range(pairs):
            roped = norm_rope_pair(
                projected_ref[here, pl.ds(pair * lanes, lanes)],
                query_gains,
                cosine,
                sine,
                head_dim,
            )
            scaled = roped.astype(jnp.bfloat16).astype(jnp.float32) * scale
            low = lanes_of(scaled) < head_dim
            to_row = (old + block) * count + 2 * pair * rows
            queries_out[pl.ds(to_row, rows), :] = jnp.where(low, scaled, 0.0).astype(jnp.bfloat16)
            queries_out[pl.ds(to_row + rows, rows), :] = jnp.where(low, 0.0, scaled).astype(
                jnp.bfloat16
            )
        last = projected_ref[here, pl.ds(query_cols, lanes)]
        roped = norm_rope_pair(last, key_gains, cosine, sine, head_dim)
        keyval_out[pl.ds((old + block) * rows, rows), :] = jnp.where(
            lanes_of(last) < head_dim, roped, last
        ).astype(jnp.bfloat16)

    keyval = keyval_out[...].astype(jnp.float32)
    low = lanes_of(keyval) < head_dim
    new_keys_ref[...] = jnp.where(low, keyval, pltpu.roll(keyval, head_dim, 1)).astype(jnp.bfloat16)
    new_values_ref[...] = jnp.where(low, 1.0, keyval).astype(jnp.bfloat16)

    token = lax.broadcasted_iota(jnp.int32, (1, blocks * rows), 1)
    key_token = token % rows + ids[0] * rows
    for block in range(1, blocks):
        key_token = jnp.where(token // rows == block, token % rows + ids[block] * rows, key_token)
    row_token = lax.broadcasted_iota(jnp.int32, (count, 1), 0) % rows

    def first_token(block, low_block, high_block):
        found = ids[low_block]
        for other in range(low_block + 1, high_block):
            found = jnp.where(block == other, ids[other], found)
        return found * rows

    def attend_new(block, unused):
        span = pl.ds(pl.multiple_of(block * count, count), count)
        queries = queries_out[span, :]
        at = first_token(block, old, blocks) + row_token
        scores = jnp.dot(queries, keys_ref[...], preferred_element_type=jnp.float32)
        masked = jnp.where(reach_ref[...] > length + at - window_len, scores, masked_score)
        near_scores = lax.dot_general(
            queries,
            new_keys_ref[...],
            (((1,), (1,)), ((), ())),
            preferred_element_type=jnp.float32,
        )
        near_masked = jnp.where(key_token <= at, near_scores, masked_score)
        row_max = jnp.maximum(
            jnp.max(masked, axis=1, keepdims=True),
            jnp.max(near_masked, axis=1, keepdims=True),
        )
        unnormed = jnp.exp(masked - row_max).astype(jnp.bfloat16)
        near_unnormed = jnp.exp(near_masked - row_max).astype(jnp.bfloat16)
        sums = jnp.dot(
            unnormed, values_ref[...], preferred_element_type=jnp.float32
        ) + jnp.dot(near_unnormed, new_values_ref[...], preferred_element_type=jnp.float32)
        stats_out[span, :] = jnp.where(lanes_of(sums) == 0, row_max, sums)
        return unused

    lax.fori_loop(old, blocks, attend_new, 0)

    def attend_old(block, unused):
        span = pl.ds(pl.multiple_of(block * count, count), count)
        at = first_token(block, 0, old) + row_token
        near_scores = lax.dot_general(
            queries_in[span, :],
            new_keys_ref[pl.ds(old * rows, fresh_blocks * rows), :],
            (((1,), (1,)), ((), ())),
            preferred_element_type=jnp.float32,
        )
        near_masked = jnp.where(key_token[:, old * rows :] <= at, near_scores, masked_score)
        before = stats_in[span, :]
        old_max = before[:, 0:1]
        before = jnp.where(lanes_of(before) == 0, before[:, 1:2], before)
        row_max = jnp.maximum(jnp.max(near_masked, axis=1, keepdims=True), old_max)
        unnormed = jnp.exp(near_masked - row_max).astype(jnp.bfloat16)
        sums = before * jnp.exp(old_max - row_max) + jnp.dot(
            unnormed,
            new_values_ref[pl.ds(old * rows, fresh_blocks * rows), :],
            preferred_element_type=jnp.float32,
        )
        stats_out[span, :] = jnp.where(lanes_of(sums) == 0, row_max, sums)
        return unused

    if old:
        lax.fori_loop(0, old, attend_old, 0)

    if final:
        for block in range(blocks):
            target = pl.ds(pl.multiple_of(ids[block] * rows, rows), rows)
            fresh_out[target, :] = keyval_out[pl.ds(block * rows, rows), :]
            for pair in range(pairs):
                joined = []
                for head in range(2):
                    from_row = block * count + (2 * pair + head) * rows
                    sums = stats_out[pl.ds(from_row, rows), :]
                    joined.append(sums / sums[:, 1:2])
                heads_out[target, pl.ds(pair * lanes, lanes)] = jnp.where(
                    lanes_of(joined[1]) < head_dim,
                    pltpu.roll(joined[0], head_dim, 1),
                    joined[1],
                ).astype(jnp.bfloat16)


def output_kernel(piece_count, heads_ref, *refs):
    weights = refs[:piece_count]
    attended, total = refs[piece_count:]
    step = pl.program_id(0)

    @pl.when(step == 0)
    def _():
        total[...] = jnp.zeros_like(total)

    for piece in range(piece_count):
        total[piece] += jnp.dot(
            heads_ref[0], weights[piece][...], preferred_element_type=jnp.float32
        )

    @pl.when(step == pl.num_programs(0) - 1)
    def _():
        width = weights[0].shape[1]
        for piece in range(piece_count):
            start = pl.multiple_of((lax.axis_index("dp") ^ piece) * width, width)
            attended[:, pl.ds(start, width)] = total[piece].astype(attended.dtype)


def whole_vmem():
    return pl.BlockSpec(memory_space=pltpu.VMEM)


def in_smem():
    return pl.BlockSpec(memory_space=pltpu.SMEM)


def run_stage(plan, final, lengths, windows, tokens, shared, weights, state):
    rows = plan["rows"]
    head_dim = plan["head_dim"]
    old, fresh_blocks = plan["old"], len(plan["parts"])
    blocks = old + fresh_blocks
    lanes = 2 * head_dim
    width = weights[0].shape[1]
    query_cols = width - lanes
    count = rows * query_cols // head_dim
    features = tokens[0].shape[1]
    slots = shared[-1].shape[1]
    state_shapes = [
        ((blocks * count, lanes), jnp.bfloat16),
        ((blocks * rows, lanes), jnp.bfloat16),
        ((blocks * count, lanes), jnp.float32),
    ]
    scratch = [
        pltpu.VMEM((fresh_blocks * rows, features), jnp.bfloat16),
        pltpu.VMEM((fresh_blocks * rows, width), jnp.float32),
    ]
    if final:
        out_shape = (
            jax.ShapeDtypeStruct((blocks * rows, query_cols), jnp.bfloat16),
            jax.ShapeDtypeStruct((blocks * rows, lanes), jnp.bfloat16),
        )
        scratch += [pltpu.VMEM(*one) for one in state_shapes]
    else:
        out_shape = tuple(jax.ShapeDtypeStruct(*one) for one in state_shapes)
    scratch += [pltpu.VMEM((blocks * rows, lanes), jnp.bfloat16)] * 2
    operands = [*tokens, *shared, *weights, *state]
    return pl.pallas_call(
        functools.partial(stage_kernel, plan, final),
        out_shape=out_shape,
        in_specs=[in_smem()] * 2 + [whole_vmem()] * len(operands),
        out_specs=(whole_vmem(),) * len(out_shape),
        scratch_shapes=scratch,
        compiler_params=pltpu.CompilerParams(vmem_limit_bytes=vmem_bytes),
        cost_estimate=pl.CostEstimate(
            flops=2 * fresh_blocks * rows * features * width
            + 16 * fresh_blocks * count * slots * lanes,
            bytes_accessed=4 * 1024 * 1024,
            transcendentals=fresh_blocks * count * slots,
        ),
    )(lengths, windows, *operands)


def body(
    tokens,
    norm_gain,
    query_weight,
    keyval_weight,
    query_gain,
    key_gain,
    output_weight,
    keyval_cache,
    cached_lengths,
    sink_count,
    window,
):
    tensor_rank = lax.axis_index("tensor")
    tensor_size = lax.axis_size("tensor")
    dp_size = lax.axis_size("dp")
    head_dim = query_gain.shape[0]
    kv_heads = keyval_weight.shape[2] // head_dim
    member = tensor_rank % kv_heads
    request_slot = tensor_rank // kv_heads
    length = cached_lengths[request_slot]
    sink_total = sink_count[request_slot]
    block_cols = query_weight.shape[1] // kv_heads
    rows = tokens.shape[0]
    new_rows = rows * kv_heads

    if tensor_size == kv_heads == 8:
        ring = [0, 2, 4, 6, 7, 5, 3, 1]
    else:
        ring = list(range(kv_heads))
    def ring_route(step):
        route = []
        for group in range(0, tensor_size, kv_heads):
            for place in range(kv_heads):
                route.append(
                    (group + ring[place], group + ring[(place + step) % kv_heads])
                )
        return route

    def forward(block):
        return lax.ppermute(block, "tensor", ring_route(1))

    def backward(block):
        return lax.ppermute(block, "tensor", ring_route(-1))

    def from_dp(block, apart):
        return lax.ppermute(block, "dp", [(one, one ^ apart) for one in range(dp_size)])

    query_local = lax.dynamic_slice_in_dim(query_weight, member * block_cols, block_cols, 1)
    keyval_local = lax.dynamic_slice_in_dim(keyval_weight, member * head_dim, head_dim, 2)
    combined = jnp.concatenate([query_local, keyval_local[0], keyval_local[1]], axis=1)
    far = dp_size // 2
    pieces = {0: combined}
    apart = far
    while apart >= 1:
        for known in list(pieces):
            pieces[known ^ apart] = from_dp(pieces[known], apart)
        apart //= 2
    weights = [pieces[k] for k in range(dp_size)]

    positions = length + jnp.arange(new_rows, dtype=jnp.int32)
    cosine, sine = rope_tables(positions, head_dim)
    cache_rows = keyval_cache[0]
    slots = cache_rows.shape[0]
    key_columns = cache_rows[:, :head_dim].T
    keys = jnp.concatenate([key_columns, key_columns], axis=0)
    values = jnp.concatenate(
        [jnp.ones((slots, head_dim), jnp.bfloat16), cache_rows[:, head_dim:]], axis=1
    )
    slot = jnp.arange(slots, dtype=jnp.int32)
    far_away = jnp.int32(1 << 29)
    reach = jnp.where(slot < length, jnp.where(slot < sink_total, far_away, slot), -far_away)
    shared = (
        norm_gain[None],
        query_gain[None],
        key_gain[None],
        cosine,
        sine,
        keys,
        values,
        reach[None],
    )

    def after(value, *others):
        return lax.optimization_barrier((value, *others))[0]

    ahead, behind = tokens, tokens
    arrived, arrived_offsets = [tokens], [0]
    offsets = []
    state = ()
    steps = (kv_heads - 1) // 2
    for step in range(1, steps + 2):
        final = step > steps
        if final:
            half = rows // 2
            arrived = [forward(ahead[:half]), backward(behind[half:])]
            arrived_offsets = [step]
            parts = (2,)
        else:
            ahead, behind = forward(ahead), backward(behind)
            arrived += [ahead, behind]
            arrived_offsets += [-step, step]
            parts = (1,) * len(arrived)
        if step == 1:
            far_out = from_dp(after(output_weight, pieces[far], ahead, behind), far)
        offsets += arrived_offsets
        plan = {
            "old": len(offsets) - len(parts),
            "offsets": tuple(offsets),
            "parts": parts,
            "pieces": dp_size,
            "head_dim": head_dim,
            "ring": tuple(ring),
            "rows": rows,
        }
        state = run_stage(
            plan, final, cached_lengths, window, arrived, shared, weights, state
        )
        if step == steps:
            out_pieces = {0: output_weight, far: after(far_out, *state)}
        arrived, arrived_offsets = [], []
    head_out, fresh = state
    apart = far // 2
    while apart >= 1:
        for known in list(out_pieces):
            out_pieces[known ^ apart] = from_dp(out_pieces[known], apart)
        apart //= 2
    out_weights = [out_pieces[k] for k in range(dp_size)]

    groups = [
        list(range(group, group + kv_heads)) for group in range(0, tensor_size, kv_heads)
    ]
    parts = lax.all_to_all(
        head_out.reshape(kv_heads, rows, block_cols),
        "tensor",
        0,
        0,
        axis_index_groups=groups,
    )
    width = output_weight.shape[1]
    attended = pl.pallas_call(
        functools.partial(output_kernel, dp_size),
        grid=(kv_heads,),
        out_shape=jax.ShapeDtypeStruct((rows, width * dp_size), jnp.bfloat16),
        in_specs=[
            pl.BlockSpec((1, rows, block_cols), lambda step: (step, 0, 0)),
        ]
        + [pl.BlockSpec((block_cols, width), lambda step: (step, 0))] * dp_size,
        out_specs=pl.BlockSpec((rows, width * dp_size), lambda step: (0, 0)),
        scratch_shapes=[pltpu.VMEM((dp_size, rows, width), jnp.float32)],
        compiler_params=pltpu.CompilerParams(vmem_limit_bytes=vmem_bytes),
    )(parts, *out_weights)
    return (attended, fresh[None])


def solution(mesh):
    in_specs = (
        P(("dp", "tensor"), None),
        P(),
        P("dp", None),
        P(None, "dp", None),
        P(),
        P(),
        P(None, "dp"),
        P(("dp", "tensor"), None, None),
        P("dp"),
        P("dp"),
        P("dp"),
    )
    out_specs = (P(("dp", "tensor"), None), P(("dp", "tensor"), None, None))
    return jax.shard_map(body, mesh=mesh, in_specs=in_specs, out_specs=out_specs, check_vma=False)
```

```python
import functools

import jax
import jax.numpy as jnp
from jax import lax
from jax.experimental import pallas as pl
from jax.experimental.pallas import tpu as pltpu
from jax.sharding import PartitionSpec as P

epsilon = 1e-05
theta_base = 1000000.0
masked_score = -1e30
vmem_bytes = 48 * 1024 * 1024


def lanes_of(value):
    return lax.broadcasted_iota(jnp.int32, value.shape, value.ndim - 1)


def norm_rope(head, gain, cosine, sine):
    mean_square = jnp.mean(head * head, axis=0, keepdims=True)
    normed = head * lax.rsqrt(mean_square + epsilon) * gain
    half_dim = head.shape[0] // 2
    first, second = normed[:half_dim], normed[half_dim:]
    return jnp.concatenate(
        [first * cosine - second * sine, second * cosine + first * sine], axis=0
    )


def table_entry(table, index):
    found = jnp.int32(table[0])
    for place in range(1, len(table)):
        found = jnp.where(index == place, jnp.int32(table[place]), found)
    return found


def stage_kernel(plan, final, length_ref, window_ref, sink_ref, *refs):
    old, offsets, parts = plan["old"], plan["offsets"], plan["parts"]
    pieces, head_dim, ring = plan["pieces"], plan["head_dim"], plan["ring"]
    members = len(ring)
    refs = list(refs)

    def take(count):
        taken = refs[:count]
        del refs[:count]
        return taken

    tokens = take(sum(parts))
    norm_gain, query_gain, key_gain, freq_ref, cache_ref, values_ref = take(6)
    weights = take(pieces)
    if old:
        queries_in, keyval_in, stats_in = take(3)
    if final:
        heads_out = take(members // 2)
        fresh_out = take(1)[0]
    else:
        queries_out, keyval_out, stats_out = take(3)
    normed_ref, projected_ref = take(2)
    if final:
        queries_out, keyval_out, stats_out, joined_ref = take(4)

    fresh_blocks = len(parts)
    blocks = old + fresh_blocks
    rows = normed_ref.shape[0] // fresh_blocks
    lanes = 2 * head_dim
    query_cols = projected_ref.shape[1] - lanes
    heads = query_cols // head_dim
    count = heads * rows
    rank = lax.axis_index("tensor")
    own = lax.axis_index("dp")
    slot = rank // members if length_ref.shape[0] > 1 else 0
    length = length_ref[slot]
    window_len = window_ref[slot]
    sink_total = sink_ref[slot]
    place = table_entry([ring.index(one) for one in range(members)], rank % members)
    ids = [table_entry(ring, (place + offset + members) % members) for offset in offsets]

    gain = norm_gain[...].astype(jnp.float32)
    start = 0
    for part in tokens:
        values = part[...].astype(jnp.float32)
        mean_square = jnp.mean(values * values, axis=1, keepdims=True)
        normed_ref[pl.ds(start, part.shape[0]), :] = (
            values * lax.rsqrt(mean_square + epsilon) * gain
        ).astype(jnp.bfloat16)
        start += part.shape[0]
    depth = weights[0].shape[0]
    total = None
    for piece in range(pieces):
        from_column = pl.multiple_of((own ^ piece) * depth, depth)
        term = jnp.dot(
            normed_ref[:, pl.ds(from_column, depth)],
            weights[piece][...],
            preferred_element_type=jnp.float32,
        )
        total = term if total is None else total + term
    projected_ref[...] = total
    scale = head_dim ** (-0.5)

    if old:
        queries_out[:, pl.ds(0, old * count)] = queries_in[...]
        keyval_out[pl.ds(0, old * rows), :] = keyval_in[...]
    padding = jnp.zeros((head_dim, count), jnp.bfloat16)
    for block in range(fresh_blocks):
        position = length + ids[old + block] * rows + lax.broadcasted_iota(jnp.int32, (1, rows), 1)
        angles = position.astype(jnp.float32) * freq_ref[...]
        cosine, sine = jnp.cos(angles), jnp.sin(angles)
        here = pl.ds(block * rows, rows)
        turned = projected_ref[here, :].T
        roped = [
            norm_rope(
                turned[head * head_dim : (head + 1) * head_dim],
                query_gain[...] if head < heads else key_gain[...],
                cosine,
                sine,
            )
            for head in range(heads + 1)
        ]
        queries = jnp.concatenate(roped[:heads], axis=1).astype(jnp.bfloat16)
        queries = (queries.astype(jnp.float32) * scale).astype(jnp.bfloat16)
        queries_out[:, pl.ds((old + block) * count, count)] = jnp.concatenate(
            [queries, padding], axis=0
        )
        keys = jnp.concatenate([roped[heads], roped[heads]], axis=0).T
        last = projected_ref[here, pl.ds(query_cols, lanes)]
        keyval_out[pl.ds((old + block) * rows, rows), :] = jnp.where(
            lanes_of(last) < head_dim, keys, last
        ).astype(jnp.bfloat16)

    turned = keyval_out[...].astype(jnp.float32).T
    new_values = jnp.where(
        lax.broadcasted_iota(jnp.int32, turned.shape, 0) < head_dim, 1.0, turned
    ).astype(jnp.bfloat16)

    def token_rows(low_block, high_block):
        step = lax.broadcasted_iota(jnp.int32, (rows, 1), 0)
        return jnp.concatenate(
            [step + ids[block] * rows for block in range(low_block, high_block)], axis=0
        )

    lane_token = lax.broadcasted_iota(jnp.int32, (1, count), 1) % rows

    def pack(row_max, sums):
        return jnp.concatenate(
            [
                jnp.broadcast_to(row_max, (8, row_max.shape[1])),
                sums[:8],
                sums[head_dim:],
            ],
            axis=0,
        )

    cache_slots = cache_ref.shape[0]
    key_token = token_rows(0, blocks)

    def attend_new(block, unused):
        span = pl.ds(pl.multiple_of(block * count, count), count)
        queries = queries_out[:, span]
        first = ids[old]
        for other in range(old + 1, blocks):
            first = jnp.where(block == other, ids[other], first)
        at = first * rows + lane_token
        scores = jnp.dot(cache_ref[...], queries, preferred_element_type=jnp.float32)
        cached = lax.broadcasted_iota(jnp.int32, (cache_slots, 1), 0)
        far_away = jnp.int32(1 << 29)
        reach = jnp.where(
            cached < length, jnp.where(cached < sink_total, far_away, cached), -far_away
        )
        masked = jnp.where(reach > length - window_len + at, scores, masked_score)
        near_scores = jnp.dot(keyval_out[...], queries, preferred_element_type=jnp.float32)
        near_masked = jnp.where(key_token <= at, near_scores, masked_score)
        row_max = jnp.maximum(
            jnp.max(masked, axis=0, keepdims=True),
            jnp.max(near_masked, axis=0, keepdims=True),
        )
        unnormed = jnp.exp(masked - row_max).astype(jnp.bfloat16)
        near_unnormed = jnp.exp(near_masked - row_max).astype(jnp.bfloat16)
        sums = jnp.dot(
            values_ref[...], unnormed, preferred_element_type=jnp.float32
        ) + jnp.dot(new_values, near_unnormed, preferred_element_type=jnp.float32)
        stats_out[:, span] = pack(row_max, sums)
        return unused

    lax.fori_loop(old, blocks, attend_new, 0)

    if old:
        span = pl.ds(0, old * count)
        at = jnp.concatenate([lane_token + ids[block] * rows for block in range(old)], axis=1)
        near_scores = jnp.dot(
            keyval_out[pl.ds(old * rows, fresh_blocks * rows), :],
            queries_in[...],
            preferred_element_type=jnp.float32,
        )
        near_masked = jnp.where(token_rows(old, blocks) <= at, near_scores, masked_score)
        old_max = stats_in[0:1, :]
        row_max = jnp.maximum(jnp.max(near_masked, axis=0, keepdims=True), old_max)
        unnormed = jnp.exp(near_masked - row_max).astype(jnp.bfloat16)
        sums = jnp.dot(
            new_values[:, old * rows :], unnormed, preferred_element_type=jnp.float32
        )
        before = stats_in[...] * jnp.exp(old_max - row_max)
        stats_out[:, span] = pack(row_max, sums) + jnp.where(
            lax.broadcasted_iota(jnp.int32, before.shape, 0) < 8, 0.0, before
        )

    if final:
        for block in range(blocks):
            target = pl.ds(pl.multiple_of(ids[block] * rows, rows), rows)
            fresh_out[target, :] = keyval_out[pl.ds(block * rows, rows), :]
            sums = stats_out[:, pl.ds(block * count, count)]
            result = sums[16:] / sums[8:9]
            pair = (ids[block] // 2) ^ (rank % members // 2)
            to_row = pl.multiple_of((pair * 2 + ids[block] % 2) * rows, rows)
            joined_ref[pl.ds(to_row, rows), :] = jnp.concatenate(
                [result[:, head * rows : (head + 1) * rows] for head in range(heads)], axis=0
            ).T.astype(jnp.bfloat16)
        for pair in range(members // 2):
            heads_out[pair][...] = joined_ref[pl.ds(pair * 2 * rows, 2 * rows), :]


def output_kernel(members, pieces, *refs):
    parts = refs[: members // 2]
    weights = refs[members // 2 : members // 2 + pieces]
    kept_ref, sent_ref, total_ref = refs[members // 2 + pieces :]
    rows, depth = kept_ref.shape[0], parts[0].shape[1]
    width = weights[0].shape[1]
    member = lax.axis_index("tensor") % members
    own = lax.axis_index("dp")
    for piece in range(pieces):
        total = None
        for pair in range(members // 2):
            from_row = pl.multiple_of(((member // 2) ^ pair) * depth, depth)
            term = jnp.dot(
                parts[pair][...],
                weights[piece][pl.ds(from_row, depth), :],
                preferred_element_type=jnp.float32,
            )
            total = term if total is None else total + term
        total_ref[...] = total
        columns = pl.ds(pl.multiple_of((own ^ piece) * width, width), width)
        mine = pl.multiple_of(member % 2 * rows, rows)
        kept_ref[:, columns] = total_ref[pl.ds(mine, rows), :]
        sent_ref[:, columns] = total_ref[pl.ds(rows - mine, rows), :].astype(sent_ref.dtype)


def whole_vmem():
    return pl.BlockSpec(memory_space=pltpu.VMEM)


def in_smem():
    return pl.BlockSpec(memory_space=pltpu.SMEM)


def run_stage(plan, final, limits, tokens, shared, weights, state):
    rows = plan["rows"]
    head_dim = plan["head_dim"]
    old, fresh_blocks = plan["old"], len(plan["parts"])
    blocks = old + fresh_blocks
    lanes = 2 * head_dim
    width = weights[0].shape[1]
    query_cols = width - lanes
    count = rows * query_cols // head_dim
    features = tokens[0].shape[1]
    slots = shared[-1].shape[1]
    state_shapes = [
        ((lanes, blocks * count), jnp.bfloat16),
        ((blocks * rows, lanes), jnp.bfloat16),
        ((head_dim + 16, blocks * count), jnp.float32),
    ]
    scratch = [
        pltpu.VMEM((fresh_blocks * rows, features), jnp.bfloat16),
        pltpu.VMEM((fresh_blocks * rows, width), jnp.float32),
    ]
    if final:
        out_shape = (
            *[jax.ShapeDtypeStruct((2 * rows, query_cols), jnp.bfloat16)] * (blocks // 2),
            jax.ShapeDtypeStruct((blocks * rows, lanes), jnp.bfloat16),
        )
        scratch += [pltpu.VMEM(*one) for one in state_shapes]
        scratch += [pltpu.VMEM((blocks * rows, query_cols), jnp.bfloat16)]
    else:
        out_shape = tuple(jax.ShapeDtypeStruct(*one) for one in state_shapes)
    operands = [*tokens, *shared, *weights, *state]
    return pl.pallas_call(
        functools.partial(stage_kernel, plan, final),
        out_shape=out_shape,
        in_specs=[in_smem()] * len(limits) + [whole_vmem()] * len(operands),
        out_specs=(whole_vmem(),) * len(out_shape),
        scratch_shapes=scratch,
        compiler_params=pltpu.CompilerParams(vmem_limit_bytes=vmem_bytes),
        cost_estimate=pl.CostEstimate(
            flops=2 * fresh_blocks * rows * features * width
            + 16 * fresh_blocks * count * slots * lanes,
            bytes_accessed=4 * 1024 * 1024,
            transcendentals=fresh_blocks * count * slots,
        ),
    )(*limits, *operands)


def body(
    tokens,
    norm_gain,
    query_weight,
    keyval_weight,
    query_gain,
    key_gain,
    output_weight,
    keyval_cache,
    cached_lengths,
    sink_count,
    window,
):
    tensor_rank = lax.axis_index("tensor")
    tensor_size = lax.axis_size("tensor")
    dp_size = lax.axis_size("dp")
    head_dim = query_gain.shape[0]
    kv_heads = keyval_weight.shape[2] // head_dim
    member = tensor_rank % kv_heads
    block_cols = query_weight.shape[1] // kv_heads
    rows = tokens.shape[0]

    if tensor_size == kv_heads == 8:
        ring = [0, 2, 4, 6, 7, 5, 3, 1]
    else:
        ring = list(range(kv_heads))
    def ring_route(step):
        route = []
        for group in range(0, tensor_size, kv_heads):
            for place in range(kv_heads):
                route.append(
                    (group + ring[place], group + ring[(place + step) % kv_heads])
                )
        return route

    def forward(block):
        return lax.ppermute(block, "tensor", ring_route(1))

    def backward(block):
        return lax.ppermute(block, "tensor", ring_route(-1))

    def from_dp(block, apart):
        return lax.ppermute(block, "dp", [(one, one ^ apart) for one in range(dp_size)])

    query_local = lax.dynamic_slice_in_dim(query_weight, member * block_cols, block_cols, 1)
    keyval_local = lax.dynamic_slice_in_dim(keyval_weight, member * head_dim, head_dim, 2)
    combined = jnp.concatenate([query_local, keyval_local[0], keyval_local[1]], axis=1)
    far = dp_size // 2
    pieces = {0: combined}
    apart = far
    while apart >= 1:
        for known in list(pieces):
            pieces[known ^ apart] = from_dp(pieces[known], apart)
        apart //= 2
    weights = [pieces[k] for k in range(dp_size)]

    half_dim = head_dim // 2
    inverse_freq = theta_base ** (-2.0 * jnp.arange(half_dim, dtype=jnp.float32) / head_dim)
    cache_rows = keyval_cache[0]
    turned = cache_rows.T
    values = jnp.where(
        lax.broadcasted_iota(jnp.int32, turned.shape, 0) < head_dim,
        jnp.ones((), jnp.bfloat16),
        turned,
    )
    shared = (
        norm_gain[None],
        query_gain[:, None],
        key_gain[:, None],
        inverse_freq[:, None],
        cache_rows,
        values,
    )
    limits = (cached_lengths, window, sink_count)

    def after(value, *others):
        return lax.optimization_barrier((value, *others))[0]

    out_local = output_weight.reshape(kv_heads // 2, 2, block_cols, -1)
    out_local = lax.dynamic_index_in_dim(out_local, member % 2, 1, keepdims=False)
    out_local = out_local.reshape(kv_heads // 2 * block_cols, -1)

    ahead, behind = tokens, tokens
    offsets = []
    state, before = (), ()
    steps = (kv_heads - 1) // 2
    for step in range(1, steps + 2):
        final = step > steps
        if before:
            ahead, behind = after(ahead, *before), after(behind, *before)
        before = state
        ahead = forward(ahead)
        if final:
            arrived, arrived_offsets = [ahead], [-step]
        else:
            behind = backward(behind)
            arrived, arrived_offsets = [ahead, behind], [-step, step]
        if step == 1:
            arrived, arrived_offsets = [tokens] + arrived, [0] + arrived_offsets
            far_out = from_dp(after(out_local, pieces[far], ahead, behind), far)
        offsets += arrived_offsets
        plan = {
            "old": len(offsets) - len(arrived),
            "offsets": tuple(offsets),
            "parts": (1,) * len(arrived),
            "pieces": dp_size,
            "head_dim": head_dim,
            "ring": tuple(ring),
            "rows": rows,
        }
        state = run_stage(plan, final, limits, arrived, shared, weights, state)
        if step == 1:
            out_pieces = {0: after(out_local, *state)}
    *head_out, fresh = state
    apart = far
    while apart >= 1:
        for known in list(out_pieces):
            if known == 0 and apart == far:
                out_pieces[far] = after(far_out, *head_out)
            else:
                out_pieces[known ^ apart] = from_dp(out_pieces[known], apart)
        apart //= 2
    out_weights = [out_pieces[k] for k in range(dp_size)]

    def from_member(block, apart):
        route = [(one, one ^ apart) for one in range(tensor_size)]
        return lax.ppermute(block, "tensor", route)

    parts = [head_out[0]] + [
        from_member(head_out[pair], 2 * pair) for pair in range(1, kv_heads // 2)
    ]
    width = output_weight.shape[1]
    kept, sent = pl.pallas_call(
        functools.partial(output_kernel, kv_heads, dp_size),
        out_shape=(
            jax.ShapeDtypeStruct((rows, width * dp_size), jnp.float32),
            jax.ShapeDtypeStruct((rows, width * dp_size), jnp.bfloat16),
        ),
        in_specs=[whole_vmem()] * (len(parts) + dp_size),
        out_specs=(whole_vmem(),) * 2,
        scratch_shapes=[pltpu.VMEM((2 * rows, width), jnp.float32)],
        compiler_params=pltpu.CompilerParams(vmem_limit_bytes=vmem_bytes),
    )(*parts, *out_weights)
    attended = (kept + from_member(sent, 1).astype(jnp.float32)).astype(jnp.bfloat16)
    return (attended, fresh[None])


def solution(mesh):
    in_specs = (
        P(("dp", "tensor"), None),
        P(),
        P("dp", None),
        P(None, "dp", None),
        P(),
        P(),
        P(None, "dp"),
        P(("dp", "tensor"), None, None),
        P("dp"),
        P("dp"),
        P("dp"),
    )
    out_specs = (P(("dp", "tensor"), None), P(("dp", "tensor"), None, None))
    return jax.shard_map(body, mesh=mesh, in_specs=in_specs, out_specs=out_specs, check_vma=False)
```

```python
import functools

import jax
import jax.numpy as jnp
import numpy as np
from jax import lax
from jax.experimental import pallas as pl
from jax.experimental.pallas import tpu as pltpu
from jax.sharding import PartitionSpec as P

epsilon = 1e-05
theta_base = 1000000.0
masked_score = -1e30
column_chunks = 4
vmem_bytes = 32 * 1024 * 1024
most_vmem_bytes = 62 * 1024 * 1024


def lanes_of(value):
    return lax.broadcasted_iota(jnp.int32, value.shape, value.ndim - 1)


def norm_rope(head, gain, cosine, sine):
    mean_square = jnp.mean(head * head, axis=0, keepdims=True)
    normed = head * lax.rsqrt(mean_square + epsilon) * gain
    half_dim = head.shape[0] // 2
    first, second = normed[:half_dim], normed[half_dim:]
    return jnp.concatenate(
        [first * cosine - second * sine, second * cosine + first * sine], axis=0
    )


def table_entry(table, index):
    found = jnp.int32(table[0])
    for place in range(1, len(table)):
        found = jnp.where(index == place, jnp.int32(table[place]), found)
    return found


def stage_kernel(plan, final, *refs):
    old, offsets, parts = plan["old"], plan["offsets"], plan["parts"]
    pieces, head_dim, ring = plan["pieces"], plan["head_dim"], plan["ring"]
    members = len(ring)
    refs = list(refs)

    def take(count):
        taken = refs[:count]
        del refs[:count]
        return taken

    limits_ref = take(1)[0]
    tokens = take(sum(parts))
    norm_gain, head_ref, cache_ref, values_ref = take(4)
    weights = take(pieces)
    if old:
        queries_in, keyval_in, stats_in = take(3)
    if final:
        heads_out = take(members // 2)
        fresh_out = take(1)[0]
    else:
        queries_out, keyval_out, stats_out = take(3)
    normed_ref, projected_ref = take(2)
    if final:
        queries_out, keyval_out, stats_out, joined_ref = take(4)

    fresh_blocks = len(parts)
    blocks = old + fresh_blocks
    rows = normed_ref.shape[0] // fresh_blocks
    lanes = 2 * head_dim
    query_cols = projected_ref.shape[1] - lanes
    heads = query_cols // head_dim
    count = heads * rows
    rank = lax.axis_index("tensor")
    own = lax.axis_index("dp")
    length = limits_ref[0:1, 0:1]
    window_len = limits_ref[1:2, 0:1]
    sink_total = limits_ref[2:3, 0:1]
    place = table_entry([ring.index(one) for one in range(members)], rank % members)
    ids = [table_entry(ring, (place + offset + members) % members) for offset in offsets]

    gain = norm_gain[...]
    start = 0
    for part in tokens:
        values = part[...].astype(jnp.float32)
        mean_square = jnp.mean(values * values, axis=1, keepdims=True)
        normed_ref[pl.ds(start, part.shape[0]), :] = (
            values * lax.rsqrt(mean_square + epsilon) * gain
        ).astype(jnp.bfloat16)
        start += part.shape[0]
    depth = weights[0].shape[0]
    total = None
    for piece in range(pieces):
        from_column = pl.multiple_of((own ^ piece) * depth, depth)
        term = jnp.dot(
            normed_ref[:, pl.ds(from_column, depth)],
            weights[piece][...],
            preferred_element_type=jnp.float32,
        )
        total = term if total is None else total + term
    projected_ref[...] = total
    scale = head_dim ** (-0.5)

    if old:
        queries_out[:, pl.ds(0, old * count)] = queries_in[...]
        keyval_out[pl.ds(0, old * rows), :] = keyval_in[...]
    padding = jnp.zeros((head_dim, count), jnp.bfloat16)
    query_gains = head_ref[:head_dim, :]
    key_gains = head_ref[head_dim : 2 * head_dim, :]
    for block in range(fresh_blocks):
        position = length + ids[old + block] * rows + lax.broadcasted_iota(jnp.int32, (1, rows), 1)
        angles = position.astype(jnp.float32) * head_ref[2 * head_dim :, :]
        cosine, sine = jnp.cos(angles), jnp.sin(angles)
        here = pl.ds(block * rows, rows)
        turned = projected_ref[here, :].T
        roped = [
            norm_rope(
                turned[head * head_dim : (head + 1) * head_dim],
                query_gains if head < heads else key_gains,
                cosine,
                sine,
            )
            for head in range(heads + 1)
        ]
        queries = jnp.concatenate(roped[:heads], axis=1).astype(jnp.bfloat16)
        queries = (queries.astype(jnp.float32) * scale).astype(jnp.bfloat16)
        queries_out[:, pl.ds((old + block) * count, count)] = jnp.concatenate(
            [queries, padding], axis=0
        )
        keys = jnp.concatenate([roped[heads], roped[heads]], axis=0).T
        last = projected_ref[here, pl.ds(query_cols, lanes)]
        keyval_out[pl.ds((old + block) * rows, rows), :] = jnp.where(
            lanes_of(last) < head_dim, keys, last
        ).astype(jnp.bfloat16)

    turned = keyval_out[...].astype(jnp.float32).T
    new_values = jnp.where(
        lax.broadcasted_iota(jnp.int32, turned.shape, 0) < head_dim, 1.0, turned
    ).astype(jnp.bfloat16)

    def token_rows(low_block, high_block):
        step = lax.broadcasted_iota(jnp.int32, (rows, 1), 0)
        return jnp.concatenate(
            [step + ids[block] * rows for block in range(low_block, high_block)], axis=0
        )

    lane_token = lax.broadcasted_iota(jnp.int32, (1, count), 1) % rows

    def pack(row_max, sums):
        return jnp.concatenate(
            [
                jnp.broadcast_to(row_max, (8, row_max.shape[1])),
                sums[:8],
                sums[head_dim:],
            ],
            axis=0,
        )

    cache_slots = cache_ref.shape[0]
    key_token = token_rows(0, blocks)

    def attend_new():
        span = pl.ds(old * count, fresh_blocks * count)
        queries = queries_out[:, span]
        at = jnp.concatenate(
            [ids[block] * rows + lane_token for block in range(old, blocks)], axis=1
        )
        scores = jnp.dot(cache_ref[...], queries, preferred_element_type=jnp.float32)
        cached = lax.broadcasted_iota(jnp.int32, (cache_slots, 1), 0)
        far_away = jnp.int32(1 << 29)
        reach = jnp.where(
            cached < length, jnp.where(cached < sink_total, far_away, cached), -far_away
        )
        masked = jnp.where(reach > length - window_len + at, scores, masked_score)
        near_scores = jnp.dot(keyval_out[...], queries, preferred_element_type=jnp.float32)
        near_masked = jnp.where(key_token <= at, near_scores, masked_score)
        row_max = jnp.maximum(
            jnp.max(masked, axis=0, keepdims=True),
            jnp.max(near_masked, axis=0, keepdims=True),
        )
        unnormed = jnp.exp(masked - row_max).astype(jnp.bfloat16)
        near_unnormed = jnp.exp(near_masked - row_max).astype(jnp.bfloat16)
        sums = jnp.dot(
            values_ref[...], unnormed, preferred_element_type=jnp.float32
        ) + jnp.dot(new_values, near_unnormed, preferred_element_type=jnp.float32)
        stats_out[:, span] = pack(row_max, sums)

    attend_new()

    if old:
        span = pl.ds(0, old * count)
        at = jnp.concatenate([lane_token + ids[block] * rows for block in range(old)], axis=1)
        near_scores = jnp.dot(
            keyval_out[pl.ds(old * rows, fresh_blocks * rows), :],
            queries_in[...],
            preferred_element_type=jnp.float32,
        )
        near_masked = jnp.where(token_rows(old, blocks) <= at, near_scores, masked_score)
        old_max = stats_in[0:1, :]
        row_max = jnp.maximum(jnp.max(near_masked, axis=0, keepdims=True), old_max)
        unnormed = jnp.exp(near_masked - row_max).astype(jnp.bfloat16)
        sums = jnp.dot(
            new_values[:, old * rows :], unnormed, preferred_element_type=jnp.float32
        )
        before = stats_in[...] * jnp.exp(old_max - row_max)
        stats_out[:, span] = pack(row_max, sums) + jnp.where(
            lax.broadcasted_iota(jnp.int32, before.shape, 0) < 8, 0.0, before
        )

    if final:
        for block in range(blocks):
            target = pl.ds(pl.multiple_of(ids[block] * rows, rows), rows)
            fresh_out[target, :] = keyval_out[pl.ds(block * rows, rows), :]
            sums = stats_out[:, pl.ds(block * count, count)]
            result = sums[16:] * (1.0 / sums[8:9])
            pair = (ids[block] // 2) ^ (rank % members // 2)
            to_row = pl.multiple_of((pair * 2 + ids[block] % 2) * rows, rows)
            joined_ref[pl.ds(to_row, rows), :] = jnp.concatenate(
                [result[:, head * rows : (head + 1) * rows] for head in range(heads)], axis=0
            ).T.astype(jnp.bfloat16)
        for pair in range(members // 2):
            heads_out[pair][...] = joined_ref[pl.ds(pair * 2 * rows, 2 * rows), :]


def output_kernel(members, held, *refs):
    parts = refs[: members // 2]
    weights = refs[members // 2 : members // 2 + len(held)]
    kept_ref, sent_ref, total_ref = refs[members // 2 + len(held) :]
    rows, depth = kept_ref.shape[0], parts[0].shape[1]
    width = weights[0].shape[1]
    member = lax.axis_index("tensor") % members
    own = lax.axis_index("dp")
    for place, piece in enumerate(held):
        total = None
        for pair in range(members // 2):
            from_row = pl.multiple_of(((member // 2) ^ pair) * depth, depth)
            term = jnp.dot(
                parts[pair][...],
                weights[place][pl.ds(from_row, depth), :],
                preferred_element_type=jnp.float32,
            )
            total = term if total is None else total + term
        total_ref[...] = total
        columns = pl.ds(pl.multiple_of((own ^ piece) % len(held) * width, width), width)
        mine = pl.multiple_of(member % 2 * rows, rows)
        kept_ref[:, columns] = total_ref[pl.ds(mine, rows), :]
        sent_ref[:, columns] = total_ref[pl.ds(rows - mine, rows), :].astype(sent_ref.dtype)


def columns_kernel(members, query_ref, keyval_ref, combined_ref, sides_ref, sems):
    member = lax.axis_index("tensor") % members
    query_cols = query_ref.shape[1] // members
    lanes = combined_ref.shape[1] - query_cols
    from_column = pl.multiple_of(member * query_cols, query_cols)
    pair_column = pl.multiple_of(member // 2 * lanes, lanes)
    depth = query_ref.shape[0]
    chunk = depth // column_chunks
    query_copies, side_copies = [], []
    for part in range(column_chunks):
        some = pl.ds(part * chunk, chunk)
        for side in range(2):
            side_copies.append(
                pltpu.make_async_copy(
                    keyval_ref.at[side, some, pl.ds(pair_column, lanes)],
                    sides_ref.at[side, some],
                    sems.at[side, part],
                )
            )
        query_copies.append(
            pltpu.make_async_copy(
                query_ref.at[some, pl.ds(from_column, query_cols)],
                combined_ref.at[some, pl.ds(0, query_cols)],
                sems.at[2, part],
            )
        )
    copies = side_copies + query_copies
    for copy in copies:
        copy.start()
    for copy in side_copies:
        copy.wait()
    keys, values = sides_ref[0], sides_ref[1]
    head_dim = lanes // 2
    even = member % 2 == 0
    low = lanes_of(keys) < head_dim

    def turned(side):
        return pltpu.roll(side.astype(jnp.float32), head_dim, 1).astype(jnp.bfloat16)

    @pl.when(even)
    def _():
        combined_ref[:, query_cols:] = jnp.where(low, keys, turned(values))

    @pl.when(jnp.logical_not(even))
    def _():
        combined_ref[:, query_cols:] = jnp.where(low, turned(keys), values)

    for copy in query_copies:
        copy.wait()


def join_kernel(near_kept, near_came, far_kept, far_came, attended_ref):
    width = near_kept.shape[1]
    side = lax.axis_index("dp") // (lax.axis_size("dp") // 2)
    for place, (kept, came) in enumerate(((near_kept, near_came), (far_kept, far_came))):
        start = pl.multiple_of((side ^ place) * width, width)
        attended_ref[:, pl.ds(start, width)] = (
            kept[...] + came[...].astype(jnp.float32)
        ).astype(attended_ref.dtype)


def turn_kernel(members, length_ref, window_ref, sink_ref, *refs):
    cache_ref, norm_gain, query_gain, key_gain, freq_ref = refs[:5]
    values_ref, gain_ref, head_ref, limits_ref = refs[7:]
    turned = cache_ref[0].astype(jnp.float32).T
    row = lax.broadcasted_iota(jnp.int32, turned.shape, 0)
    head_dim = turned.shape[0] // 2
    values_ref[...] = jnp.where(row < head_dim, 1.0, turned).astype(jnp.bfloat16)
    gain = norm_gain[...].astype(jnp.float32)
    gain_ref[...] = jnp.concatenate([gain[one : one + 1] for one in range(gain.shape[0])], axis=1)
    rows = head_ref.shape[1]
    for place, one in enumerate((query_gain, key_gain)):
        head_ref[pl.ds(place * head_dim, head_dim), :] = jnp.broadcast_to(
            one[...], (rows, head_dim)
        ).T
    head_ref[pl.ds(2 * head_dim, head_dim // 2), :] = freq_ref[...]
    slot = lax.axis_index("tensor") // members if length_ref.shape[0] > 1 else 0
    line = lax.broadcasted_iota(jnp.int32, limits_ref.shape, 0)
    limits_ref[...] = jnp.where(
        line == 0, length_ref[slot], jnp.where(line == 1, window_ref[slot], sink_ref[slot])
    )


def whole_vmem():
    return pl.BlockSpec(memory_space=pltpu.VMEM)


def run_stage(plan, final, limits, tokens, shared, weights, state):
    rows = plan["rows"]
    head_dim = plan["head_dim"]
    old, fresh_blocks = plan["old"], len(plan["parts"])
    blocks = old + fresh_blocks
    lanes = 2 * head_dim
    width = weights[0].shape[1]
    query_cols = width - lanes
    count = rows * query_cols // head_dim
    features = tokens[0].shape[1]
    slots = shared[-1].shape[1]
    state_shapes = [
        ((lanes, blocks * count), jnp.bfloat16),
        ((blocks * rows, lanes), jnp.bfloat16),
        ((head_dim + 16, blocks * count), jnp.float32),
    ]
    scratch = [
        pltpu.VMEM((fresh_blocks * rows, features), jnp.bfloat16),
        pltpu.VMEM((fresh_blocks * rows, width), jnp.float32),
    ]
    if final:
        out_shape = (
            *[jax.ShapeDtypeStruct((2 * rows, query_cols), jnp.bfloat16)] * (blocks // 2),
            jax.ShapeDtypeStruct((blocks * rows, lanes), jnp.bfloat16),
        )
        scratch += [pltpu.VMEM(*one) for one in state_shapes]
        scratch += [pltpu.VMEM((blocks * rows, query_cols), jnp.bfloat16)]
    else:
        out_shape = tuple(jax.ShapeDtypeStruct(*one) for one in state_shapes)
    operands = [limits, *tokens, *shared, *weights, *state]
    return pl.pallas_call(
        functools.partial(stage_kernel, plan, final),
        out_shape=out_shape,
        in_specs=[whole_vmem()] * len(operands),
        out_specs=(whole_vmem(),) * len(out_shape),
        scratch_shapes=scratch,
        compiler_params=pltpu.CompilerParams(vmem_limit_bytes=vmem_bytes),
        cost_estimate=pl.CostEstimate(flops=1024, bytes_accessed=1024, transcendentals=0),
    )(*operands)


def body(
    tokens,
    norm_gain,
    query_weight,
    keyval_weight,
    query_gain,
    key_gain,
    output_weight,
    keyval_cache,
    cached_lengths,
    sink_count,
    window,
):
    tensor_rank = lax.axis_index("tensor")
    tensor_size = lax.axis_size("tensor")
    dp_size = lax.axis_size("dp")
    head_dim = query_gain.shape[0]
    kv_heads = keyval_weight.shape[2] // head_dim
    member = tensor_rank % kv_heads
    block_cols = query_weight.shape[1] // kv_heads
    rows = tokens.shape[0]

    if tensor_size == kv_heads == 8:
        ring = [0, 2, 4, 6, 7, 5, 3, 1]
    else:
        ring = list(range(kv_heads))
    def ring_route(step):
        route = []
        for group in range(0, tensor_size, kv_heads):
            for place in range(kv_heads):
                route.append(
                    (group + ring[place], group + ring[(place + step) % kv_heads])
                )
        return route

    def forward(block):
        return lax.ppermute(block, "tensor", ring_route(1))

    def backward(block):
        return lax.ppermute(block, "tensor", ring_route(-1))

    def from_dp(block, apart):
        return lax.ppermute(block, "dp", [(one, one ^ apart) for one in range(dp_size)])

    depth = query_weight.shape[0]
    combined = pl.pallas_call(
        functools.partial(columns_kernel, kv_heads),
        out_shape=jax.ShapeDtypeStruct((depth, block_cols + 2 * head_dim), jnp.bfloat16),
        in_specs=[pl.BlockSpec(memory_space=pltpu.HBM)] * 2,
        out_specs=whole_vmem(),
        scratch_shapes=[
            pltpu.VMEM((2, depth, 2 * head_dim), jnp.bfloat16),
            pltpu.SemaphoreType.DMA((3, column_chunks)),
        ],
        cost_estimate=pl.CostEstimate(flops=0, bytes_accessed=1 << 25, transcendentals=0),
        compiler_params=pltpu.CompilerParams(vmem_limit_bytes=most_vmem_bytes),
    )(query_weight, keyval_weight)
    far = dp_size // 2

    def after(value, *others):
        return lax.optimization_barrier((value, *others))[0]

    pieces = {0: combined, far: from_dp(combined, far)}
    steps = (kv_heads - 1) // 2
    early = min(2, steps)
    chain, chain_offsets = [tokens], [0]
    ahead, behind = tokens, tokens
    for step in range(1, early + 1):
        ahead, behind = forward(ahead), backward(behind)
        chain += [ahead, behind]
        chain_offsets += [-step, step]
    exponents = -2.0 * np.arange(head_dim // 2, dtype=np.float32) / np.float32(head_dim)
    inverse_freq = np.power(np.float32(theta_base), exponents, dtype=np.float32)
    inverse_freq = np.tile(inverse_freq[:, None], (1, rows))
    cache_rows = keyval_cache[0]
    features = norm_gain.shape[0]
    values, gain_row, head_table, limits = pl.pallas_call(
        functools.partial(turn_kernel, kv_heads),
        out_shape=(
            jax.ShapeDtypeStruct(cache_rows.shape[::-1], jnp.bfloat16),
            jax.ShapeDtypeStruct((1, features), jnp.float32),
            jax.ShapeDtypeStruct((2 * head_dim + head_dim // 2, rows), jnp.float32),
            jax.ShapeDtypeStruct((8, 128), jnp.int32),
        ),
        in_specs=[pl.BlockSpec(memory_space=pltpu.SMEM)] * 3
        + [whole_vmem()] * 5
        + [pl.BlockSpec(memory_space=pl.ANY)] * 2,
        out_specs=(whole_vmem(),) * 4,
        compiler_params=pltpu.CompilerParams(vmem_limit_bytes=vmem_bytes),
    )(
        cached_lengths,
        window,
        sink_count,
        keyval_cache,
        norm_gain.reshape(-1, 128),
        query_gain[None],
        key_gain[None],
        jnp.asarray(inverse_freq),
        *chain[1:3],
    )
    out_local = after(output_weight, *chain[1:3]).reshape(kv_heads // 2, 2, block_cols, -1)
    out_local = lax.dynamic_index_in_dim(out_local, member % 2, 1, keepdims=False)
    out_local = out_local.reshape(kv_heads // 2 * block_cols, -1)
    far_out = from_dp(after(out_local, pieces[far], values, *chain[1:]), far)
    pieces[far], values, *unused = lax.optimization_barrier((pieces[far], values, *chain[1:]))
    apart = far // 2
    while apart >= 1:
        for known in list(pieces):
            pieces[known ^ apart] = from_dp(pieces[known], apart)
        apart //= 2
    weights = [pieces[k] for k in range(dp_size)]
    shared = (
        gain_row,
        head_table,
        cache_rows,
        values,
    )

    offsets = []
    state = ()
    arrived, arrived_offsets = chain, chain_offsets
    for step in range(early + 1, steps + 3):
        final = step > steps + 1
        offsets += arrived_offsets
        plan = {
            "old": len(offsets) - len(arrived_offsets),
            "offsets": tuple(offsets),
            "parts": (2,) if final else (1,) * len(arrived),
            "pieces": dp_size,
            "head_dim": head_dim,
            "ring": tuple(ring),
            "rows": rows,
        }
        before = state
        if not final:
            if before:
                ahead, behind = after(ahead, *before), after(behind, *before)
            if step > steps:
                ahead, behind = ahead[: rows // 2], behind[rows // 2 :]
            ahead, behind = forward(ahead), backward(behind)
        state = run_stage(plan, final, limits, arrived, shared, weights, state)
        arrived = [ahead, behind]
        arrived_offsets = [-step, step] if step <= steps else [step]
        if not before:
            out_pieces = {0: after(out_local, *state)}
    *head_out, fresh = state
    def from_member(block, apart):
        route = [(one, one ^ apart) for one in range(tensor_size)]
        return lax.ppermute(block, "tensor", route)

    parts = [head_out[0]] + [
        from_member(head_out[pair], 2 * pair) for pair in range(1, kv_heads // 2)
    ]
    width = output_weight.shape[1]

    def project(held):
        return pl.pallas_call(
            functools.partial(output_kernel, kv_heads, held),
            out_shape=(
                jax.ShapeDtypeStruct((rows, width * len(held)), jnp.float32),
                jax.ShapeDtypeStruct((rows, width * len(held)), jnp.bfloat16),
            ),
            in_specs=[whole_vmem()] * (len(parts) + len(held)),
            out_specs=(whole_vmem(),) * 2,
            scratch_shapes=[pltpu.VMEM((2 * rows, width), jnp.float32)],
            compiler_params=pltpu.CompilerParams(vmem_limit_bytes=vmem_bytes),
        )(*parts, *[out_pieces[piece] for piece in held])

    def spread(known_pieces, apart):
        while apart >= 1:
            for known in known_pieces:
                out_pieces[known ^ apart] = from_dp(out_pieces[known], apart)
            known_pieces = known_pieces + [known ^ apart for known in known_pieces]
            apart //= 2

    spread([0], far // 2)
    near_kept, near_sent = project(tuple(range(far)))
    near_came = from_member(near_sent, 1)
    out_pieces[far] = after(far_out, *parts[1:])
    spread([far], far // 2)
    far_kept, far_sent = project(tuple(range(far, dp_size)))
    far_came = from_member(far_sent, 1)
    attended = pl.pallas_call(
        join_kernel,
        out_shape=jax.ShapeDtypeStruct((rows, width * dp_size), jnp.bfloat16),
        in_specs=[whole_vmem()] * 4,
        out_specs=whole_vmem(),
        compiler_params=pltpu.CompilerParams(vmem_limit_bytes=vmem_bytes),
    )(near_kept, near_came, far_kept, far_came)
    return (attended, fresh[None])


def solution(mesh):
    in_specs = (
        P(("dp", "tensor"), None),
        P(),
        P("dp", None),
        P(None, "dp", None),
        P(),
        P(),
        P(None, "dp"),
        P(("dp", "tensor"), None, None),
        P("dp"),
        P("dp"),
        P("dp"),
    )
    out_specs = (P(("dp", "tensor"), None), P(("dp", "tensor"), None, None))
    return jax.shard_map(body, mesh=mesh, in_specs=in_specs, out_specs=out_specs, check_vma=False)
```

```python
import functools

import jax
import jax.numpy as jnp
import numpy as np
from jax import lax
from jax.experimental import pallas as pl
from jax.experimental.pallas import tpu as pltpu
from jax.sharding import PartitionSpec as P

epsilon = 1e-05
theta_base = 1000000.0
masked_score = -1e30
column_chunks = 4
vmem_bytes = 32 * 1024 * 1024
most_vmem_bytes = 62 * 1024 * 1024


def lanes_of(value):
    return lax.broadcasted_iota(jnp.int32, value.shape, value.ndim - 1)


def norm_rope(head, gain, cosine, sine):
    mean_square = jnp.mean(head * head, axis=0, keepdims=True)
    normed = head * lax.rsqrt(mean_square + epsilon) * gain
    half_dim = head.shape[0] // 2
    first, second = normed[:half_dim], normed[half_dim:]
    return jnp.concatenate(
        [first * cosine - second * sine, second * cosine + first * sine], axis=0
    )


def table_entry(table, index):
    found = jnp.int32(table[0])
    for place in range(1, len(table)):
        found = jnp.where(index == place, jnp.int32(table[place]), found)
    return found


def stage_kernel(plan, final, *refs):
    old, offsets, parts = plan["old"], plan["offsets"], plan["parts"]
    pieces, head_dim, ring = plan["pieces"], plan["head_dim"], plan["ring"]
    members = len(ring)
    refs = list(refs)

    def take(count):
        taken = refs[:count]
        del refs[:count]
        return taken

    limits_ref = take(1)[0]
    tokens = take(sum(parts))
    norm_gain, head_ref, cache_ref, values_ref = take(4)
    weights = take(pieces)
    if old:
        queries_in, keyval_in, stats_in = take(3)
    if final:
        heads_out = take(members // 2)
        fresh_out = take(1)[0]
    else:
        queries_out, keyval_out, stats_out = take(3)
    normed_ref, projected_ref = take(2)
    if final:
        queries_out, keyval_out, stats_out, joined_ref = take(4)

    fresh_blocks = len(parts)
    blocks = old + fresh_blocks
    rows = normed_ref.shape[0] // fresh_blocks
    lanes = 2 * head_dim
    query_cols = projected_ref.shape[1] - lanes
    heads = query_cols // head_dim
    count = heads * rows
    rank = lax.axis_index("tensor")
    own = lax.axis_index("dp")
    length = limits_ref[0:1, 0:1]
    window_len = limits_ref[1:2, 0:1]
    sink_total = limits_ref[2:3, 0:1]
    place = table_entry([ring.index(one) for one in range(members)], rank % members)
    ids = [table_entry(ring, (place + offset + members) % members) for offset in offsets]

    gain = norm_gain[...]
    start = 0
    for part in tokens:
        values = part[...].astype(jnp.float32)
        mean_square = jnp.mean(values * values, axis=1, keepdims=True)
        normed_ref[pl.ds(start, part.shape[0]), :] = (
            values * lax.rsqrt(mean_square + epsilon) * gain
        ).astype(jnp.bfloat16)
        start += part.shape[0]
    depth = weights[0].shape[0]
    total = None
    for piece in range(pieces):
        from_column = pl.multiple_of((own ^ piece) * depth, depth)
        term = jnp.dot(
            normed_ref[:, pl.ds(from_column, depth)],
            weights[piece][...],
            preferred_element_type=jnp.float32,
        )
        total = term if total is None else total + term
    projected_ref[...] = total
    scale = head_dim ** (-0.5)

    if old and not final:
        queries_out[:, pl.ds(0, old * count)] = queries_in[...]
    if old:
        keyval_out[pl.ds(0, old * rows), :] = keyval_in[...]
    padding = jnp.zeros((head_dim, count), jnp.bfloat16)
    query_gains = head_ref[:head_dim, :]
    key_gains = head_ref[head_dim : 2 * head_dim, :]
    for block in range(fresh_blocks):
        position = length + ids[old + block] * rows + lax.broadcasted_iota(jnp.int32, (1, rows), 1)
        angles = position.astype(jnp.float32) * head_ref[2 * head_dim :, :]
        cosine, sine = jnp.cos(angles), jnp.sin(angles)
        here = pl.ds(block * rows, rows)
        turned = projected_ref[here, :].T
        roped = [
            norm_rope(
                turned[head * head_dim : (head + 1) * head_dim],
                query_gains if head < heads else key_gains,
                cosine,
                sine,
            )
            for head in range(heads + 1)
        ]
        queries = jnp.concatenate(roped[:heads], axis=1).astype(jnp.bfloat16)
        queries = (queries.astype(jnp.float32) * scale).astype(jnp.bfloat16)
        queries_out[:, pl.ds((old + block) * count, count)] = jnp.concatenate(
            [queries, padding], axis=0
        )
        keys = jnp.concatenate([roped[heads], roped[heads]], axis=0).T
        last = projected_ref[here, pl.ds(query_cols, lanes)]
        keyval_out[pl.ds((old + block) * rows, rows), :] = jnp.where(
            lanes_of(last) < head_dim, keys, last
        ).astype(jnp.bfloat16)

    turned = keyval_out[...].astype(jnp.float32).T
    new_values = jnp.where(
        lax.broadcasted_iota(jnp.int32, turned.shape, 0) < head_dim, 1.0, turned
    ).astype(jnp.bfloat16)

    def token_rows(low_block, high_block):
        step = lax.broadcasted_iota(jnp.int32, (rows, 1), 0)
        return jnp.concatenate(
            [step + ids[block] * rows for block in range(low_block, high_block)], axis=0
        )

    lane_token = lax.broadcasted_iota(jnp.int32, (1, count), 1) % rows

    def pack(row_max, sums):
        return jnp.concatenate(
            [
                jnp.broadcast_to(row_max, (8, row_max.shape[1])),
                sums[:8],
                sums[head_dim:],
            ],
            axis=0,
        )

    cache_slots = cache_ref.shape[0]
    key_token = token_rows(0, blocks)

    def attend_new():
        span = pl.ds(old * count, fresh_blocks * count)
        queries = queries_out[:, span]
        at = jnp.concatenate(
            [ids[block] * rows + lane_token for block in range(old, blocks)], axis=1
        )
        scores = jnp.dot(cache_ref[...], queries, preferred_element_type=jnp.float32)
        cached = lax.broadcasted_iota(jnp.int32, (cache_slots, 1), 0)
        far_away = jnp.int32(1 << 29)
        reach = jnp.where(
            cached < length, jnp.where(cached < sink_total, far_away, cached), -far_away
        )
        masked = jnp.where(reach > length - window_len + at, scores, masked_score)
        near_scores = jnp.dot(keyval_out[...], queries, preferred_element_type=jnp.float32)
        near_masked = jnp.where(key_token <= at, near_scores, masked_score)
        row_max = jnp.maximum(
            jnp.max(masked, axis=0, keepdims=True),
            jnp.max(near_masked, axis=0, keepdims=True),
        )
        unnormed = jnp.exp(masked - row_max).astype(jnp.bfloat16)
        near_unnormed = jnp.exp(near_masked - row_max).astype(jnp.bfloat16)
        sums = jnp.dot(
            values_ref[...], unnormed, preferred_element_type=jnp.float32
        ) + jnp.dot(new_values, near_unnormed, preferred_element_type=jnp.float32)
        stats_out[:, span] = pack(row_max, sums)

    if old:
        span = pl.ds(0, old * count)
        at = jnp.concatenate([lane_token + ids[block] * rows for block in range(old)], axis=1)
        near_scores = jnp.dot(
            keyval_out[pl.ds(old * rows, fresh_blocks * rows), :],
            queries_in[...],
            preferred_element_type=jnp.float32,
        )
        near_masked = jnp.where(token_rows(old, blocks) <= at, near_scores, masked_score)
        old_max = stats_in[0:1, :]
        row_max = jnp.maximum(jnp.max(near_masked, axis=0, keepdims=True), old_max)
        unnormed = jnp.exp(near_masked - row_max).astype(jnp.bfloat16)
        sums = jnp.dot(
            new_values[:, old * rows :], unnormed, preferred_element_type=jnp.float32
        )
        before = stats_in[...] * jnp.exp(old_max - row_max)
        stats_out[:, span] = pack(row_max, sums) + jnp.where(
            lax.broadcasted_iota(jnp.int32, before.shape, 0) < 8, 0.0, before
        )

    attend_new()

    if final:
        for block in range(blocks):
            target = pl.ds(pl.multiple_of(ids[block] * rows, rows), rows)
            fresh_out[target, :] = keyval_out[pl.ds(block * rows, rows), :]
            sums = stats_out[:, pl.ds(block * count, count)]
            result = sums[16:] * (1.0 / sums[8:9])
            pair = (ids[block] // 2) ^ (rank % members // 2)
            to_row = pl.multiple_of((pair * 2 + ids[block] % 2) * rows, rows)
            joined_ref[pl.ds(to_row, rows), :] = jnp.concatenate(
                [result[:, head * rows : (head + 1) * rows] for head in range(heads)], axis=0
            ).T.astype(jnp.bfloat16)
        for pair in range(members // 2):
            heads_out[pair][...] = joined_ref[pl.ds(pair * 2 * rows, 2 * rows), :]


def output_kernel(members, held, *refs):
    parts = refs[: members // 2]
    weights = refs[members // 2 : members // 2 + len(held)]
    kept_ref, sent_ref, total_ref = refs[members // 2 + len(held) :]
    rows, depth = kept_ref.shape[0], parts[0].shape[1]
    width = weights[0].shape[1]
    member = lax.axis_index("tensor") % members
    own = lax.axis_index("dp")
    for place, piece in enumerate(held):
        total = None
        for pair in range(members // 2):
            from_row = pl.multiple_of(((member // 2) ^ pair) * depth, depth)
            term = jnp.dot(
                parts[pair][...],
                weights[place][pl.ds(from_row, depth), :],
                preferred_element_type=jnp.float32,
            )
            total = term if total is None else total + term
        total_ref[...] = total
        columns = pl.ds(pl.multiple_of((own ^ piece) % len(held) * width, width), width)
        mine = pl.multiple_of(member % 2 * rows, rows)
        kept_ref[:, columns] = total_ref[pl.ds(mine, rows), :]
        sent_ref[:, columns] = total_ref[pl.ds(rows - mine, rows), :].astype(sent_ref.dtype)


def columns_kernel(members, query_ref, keyval_ref, combined_ref, sides_ref, sems):
    member = lax.axis_index("tensor") % members
    query_cols = query_ref.shape[1] // members
    lanes = combined_ref.shape[1] - query_cols
    from_column = pl.multiple_of(member * query_cols, query_cols)
    pair_column = pl.multiple_of(member // 2 * lanes, lanes)
    depth = query_ref.shape[0]
    chunk = depth // column_chunks
    query_copies, side_copies = [], []
    for part in range(column_chunks):
        some = pl.ds(part * chunk, chunk)
        for side in range(2):
            side_copies.append(
                pltpu.make_async_copy(
                    keyval_ref.at[side, some, pl.ds(pair_column, lanes)],
                    sides_ref.at[side, some],
                    sems.at[side, part],
                )
            )
        query_copies.append(
            pltpu.make_async_copy(
                query_ref.at[some, pl.ds(from_column, query_cols)],
                combined_ref.at[some, pl.ds(0, query_cols)],
                sems.at[2, part],
            )
        )
    copies = side_copies + query_copies
    for copy in copies:
        copy.start()
    for copy in side_copies:
        copy.wait()
    keys, values = sides_ref[0], sides_ref[1]
    head_dim = lanes // 2
    even = member % 2 == 0
    low = lanes_of(keys) < head_dim

    def turned(side):
        return pltpu.roll(side.astype(jnp.float32), head_dim, 1).astype(jnp.bfloat16)

    @pl.when(even)
    def _():
        combined_ref[:, query_cols:] = jnp.where(low, keys, turned(values))

    @pl.when(jnp.logical_not(even))
    def _():
        combined_ref[:, query_cols:] = jnp.where(low, turned(keys), values)

    for copy in query_copies:
        copy.wait()


def join_kernel(near_kept, near_came, far_kept, far_came, attended_ref):
    width = near_kept.shape[1]
    side = lax.axis_index("dp") // (lax.axis_size("dp") // 2)
    for place, (kept, came) in enumerate(((near_kept, near_came), (far_kept, far_came))):
        start = pl.multiple_of((side ^ place) * width, width)
        attended_ref[:, pl.ds(start, width)] = (
            kept[...] + came[...].astype(jnp.float32)
        ).astype(attended_ref.dtype)


def turn_kernel(members, length_ref, window_ref, sink_ref, *refs):
    cache_ref, norm_gain, query_gain, key_gain, freq_ref = refs[:5]
    values_ref, gain_ref, head_ref, limits_ref = refs[7:]
    turned = cache_ref[0].astype(jnp.float32).T
    row = lax.broadcasted_iota(jnp.int32, turned.shape, 0)
    head_dim = turned.shape[0] // 2
    values_ref[...] = jnp.where(row < head_dim, 1.0, turned).astype(jnp.bfloat16)
    gain = norm_gain[...].astype(jnp.float32)
    gain_ref[...] = jnp.concatenate([gain[one : one + 1] for one in range(gain.shape[0])], axis=1)
    rows = head_ref.shape[1]
    for place, one in enumerate((query_gain, key_gain)):
        head_ref[pl.ds(place * head_dim, head_dim), :] = jnp.broadcast_to(
            one[...], (rows, head_dim)
        ).T
    head_ref[pl.ds(2 * head_dim, head_dim // 2), :] = freq_ref[...]
    slot = lax.axis_index("tensor") // members if length_ref.shape[0] > 1 else 0
    line = lax.broadcasted_iota(jnp.int32, limits_ref.shape, 0)
    limits_ref[...] = jnp.where(
        line == 0, length_ref[slot], jnp.where(line == 1, window_ref[slot], sink_ref[slot])
    )


def whole_vmem():
    return pl.BlockSpec(memory_space=pltpu.VMEM)


def run_stage(plan, final, limits, tokens, shared, weights, state):
    rows = plan["rows"]
    head_dim = plan["head_dim"]
    old, fresh_blocks = plan["old"], len(plan["parts"])
    blocks = old + fresh_blocks
    lanes = 2 * head_dim
    width = weights[0].shape[1]
    query_cols = width - lanes
    count = rows * query_cols // head_dim
    features = tokens[0].shape[1]
    slots = shared[-1].shape[1]
    state_shapes = [
        ((lanes, blocks * count), jnp.bfloat16),
        ((blocks * rows, lanes), jnp.bfloat16),
        ((head_dim + 16, blocks * count), jnp.float32),
    ]
    scratch = [
        pltpu.VMEM((fresh_blocks * rows, features), jnp.bfloat16),
        pltpu.VMEM((fresh_blocks * rows, width), jnp.float32),
    ]
    if final:
        out_shape = (
            *[jax.ShapeDtypeStruct((2 * rows, query_cols), jnp.bfloat16)] * (blocks // 2),
            jax.ShapeDtypeStruct((blocks * rows, lanes), jnp.bfloat16),
        )
        scratch += [pltpu.VMEM(*one) for one in state_shapes]
        scratch += [pltpu.VMEM((blocks * rows, query_cols), jnp.bfloat16)]
    else:
        out_shape = tuple(jax.ShapeDtypeStruct(*one) for one in state_shapes)
    operands = [limits, *tokens, *shared, *weights, *state]
    return pl.pallas_call(
        functools.partial(stage_kernel, plan, final),
        out_shape=out_shape,
        in_specs=[whole_vmem()] * len(operands),
        out_specs=(whole_vmem(),) * len(out_shape),
        scratch_shapes=scratch,
        compiler_params=pltpu.CompilerParams(vmem_limit_bytes=vmem_bytes),
        cost_estimate=pl.CostEstimate(flops=1024, bytes_accessed=1024, transcendentals=0),
    )(*operands)


def body(
    tokens,
    norm_gain,
    query_weight,
    keyval_weight,
    query_gain,
    key_gain,
    output_weight,
    keyval_cache,
    cached_lengths,
    sink_count,
    window,
):
    tensor_rank = lax.axis_index("tensor")
    tensor_size = lax.axis_size("tensor")
    dp_size = lax.axis_size("dp")
    head_dim = query_gain.shape[0]
    kv_heads = keyval_weight.shape[2] // head_dim
    member = tensor_rank % kv_heads
    block_cols = query_weight.shape[1] // kv_heads
    rows = tokens.shape[0]

    if tensor_size == kv_heads == 8:
        ring = [0, 2, 4, 6, 7, 5, 3, 1]
    else:
        ring = list(range(kv_heads))
    def ring_route(step):
        route = []
        for group in range(0, tensor_size, kv_heads):
            for place in range(kv_heads):
                route.append(
                    (group + ring[place], group + ring[(place + step) % kv_heads])
                )
        return route

    def forward(block):
        return lax.ppermute(block, "tensor", ring_route(1))

    def backward(block):
        return lax.ppermute(block, "tensor", ring_route(-1))

    def from_dp(block, apart):
        return lax.ppermute(block, "dp", [(one, one ^ apart) for one in range(dp_size)])

    depth = query_weight.shape[0]
    combined = pl.pallas_call(
        functools.partial(columns_kernel, kv_heads),
        out_shape=jax.ShapeDtypeStruct((depth, block_cols + 2 * head_dim), jnp.bfloat16),
        in_specs=[pl.BlockSpec(memory_space=pltpu.HBM)] * 2,
        out_specs=whole_vmem(),
        scratch_shapes=[
            pltpu.VMEM((2, depth, 2 * head_dim), jnp.bfloat16),
            pltpu.SemaphoreType.DMA((3, column_chunks)),
        ],
        cost_estimate=pl.CostEstimate(flops=0, bytes_accessed=1 << 25, transcendentals=0),
        compiler_params=pltpu.CompilerParams(vmem_limit_bytes=most_vmem_bytes),
    )(query_weight, keyval_weight)
    far = dp_size // 2

    def after(value, *others):
        return lax.optimization_barrier((value, *others))[0]

    pieces = {0: combined, far: from_dp(combined, far)}
    steps = (kv_heads - 1) // 2
    early = min(2, steps)
    chain, chain_offsets = [tokens], [0]
    ahead, behind = tokens, tokens
    for step in range(1, early + 1):
        ahead, behind = forward(ahead), backward(behind)
        chain += [ahead, behind]
        chain_offsets += [-step, step]
    exponents = -2.0 * np.arange(head_dim // 2, dtype=np.float32) / np.float32(head_dim)
    inverse_freq = np.power(np.float32(theta_base), exponents, dtype=np.float32)
    inverse_freq = np.tile(inverse_freq[:, None], (1, rows))
    cache_rows = keyval_cache[0]
    features = norm_gain.shape[0]
    values, gain_row, head_table, limits = pl.pallas_call(
        functools.partial(turn_kernel, kv_heads),
        out_shape=(
            jax.ShapeDtypeStruct(cache_rows.shape[::-1], jnp.bfloat16),
            jax.ShapeDtypeStruct((1, features), jnp.float32),
            jax.ShapeDtypeStruct((2 * head_dim + head_dim // 2, rows), jnp.float32),
            jax.ShapeDtypeStruct((8, 128), jnp.int32),
        ),
        in_specs=[pl.BlockSpec(memory_space=pltpu.SMEM)] * 3
        + [whole_vmem()] * 5
        + [pl.BlockSpec(memory_space=pl.ANY)] * 2,
        out_specs=(whole_vmem(),) * 4,
        compiler_params=pltpu.CompilerParams(vmem_limit_bytes=vmem_bytes),
    )(
        cached_lengths,
        window,
        sink_count,
        keyval_cache,
        norm_gain.reshape(-1, 128),
        query_gain[None],
        key_gain[None],
        jnp.asarray(inverse_freq),
        *chain[1:3],
    )
    out_local = after(output_weight, *chain[1:3]).reshape(kv_heads // 2, 2, block_cols, -1)
    out_local = lax.dynamic_index_in_dim(out_local, member % 2, 1, keepdims=False)
    out_local = out_local.reshape(kv_heads // 2 * block_cols, -1)
    far_out = from_dp(after(out_local, pieces[far], values, *chain[1:]), far)
    pieces[far], values, *unused = lax.optimization_barrier((pieces[far], values, *chain[1:]))
    apart = far // 2
    while apart >= 1:
        for known in list(pieces):
            pieces[known ^ apart] = from_dp(pieces[known], apart)
        apart //= 2
    weights = [pieces[k] for k in range(dp_size)]
    shared = (
        gain_row,
        head_table,
        cache_rows,
        values,
    )

    offsets = []
    state = ()
    arrived, arrived_offsets = chain, chain_offsets
    for step in range(early + 1, steps + 3):
        final = step > steps + 1
        offsets += arrived_offsets
        plan = {
            "old": len(offsets) - len(arrived_offsets),
            "offsets": tuple(offsets),
            "parts": (2,) if final else (1,) * len(arrived),
            "pieces": dp_size,
            "head_dim": head_dim,
            "ring": tuple(ring),
            "rows": rows,
        }
        before = state
        if not final:
            if before:
                ahead, behind = after(ahead, *before), after(behind, *before)
            if step > steps:
                ahead, behind = ahead[: rows // 2], behind[rows // 2 :]
            ahead, behind = forward(ahead), backward(behind)
        state = run_stage(plan, final, limits, arrived, shared, weights, state)
        arrived = [ahead, behind]
        arrived_offsets = [-step, step] if step <= steps else [step]
        if not before:
            out_pieces = {0: after(out_local, *state)}
    *head_out, fresh = state
    def from_member(block, apart):
        route = [(one, one ^ apart) for one in range(tensor_size)]
        return lax.ppermute(block, "tensor", route)

    parts = [head_out[0]] + [
        from_member(head_out[pair], 2 * pair) for pair in range(1, kv_heads // 2)
    ]
    width = output_weight.shape[1]

    def project(held):
        return pl.pallas_call(
            functools.partial(output_kernel, kv_heads, held),
            out_shape=(
                jax.ShapeDtypeStruct((rows, width * len(held)), jnp.float32),
                jax.ShapeDtypeStruct((rows, width * len(held)), jnp.bfloat16),
            ),
            in_specs=[whole_vmem()] * (len(parts) + len(held)),
            out_specs=(whole_vmem(),) * 2,
            scratch_shapes=[pltpu.VMEM((2 * rows, width), jnp.float32)],
            compiler_params=pltpu.CompilerParams(vmem_limit_bytes=vmem_bytes),
        )(*parts, *[out_pieces[piece] for piece in held])

    def spread(known_pieces, apart):
        while apart >= 1:
            for known in known_pieces:
                out_pieces[known ^ apart] = from_dp(out_pieces[known], apart)
            known_pieces = known_pieces + [known ^ apart for known in known_pieces]
            apart //= 2

    spread([0], far // 2)
    near_kept, near_sent = project(tuple(range(far)))
    near_came = from_member(near_sent, 1)
    out_pieces[far] = after(far_out, *parts[1:])
    spread([far], far // 2)
    far_kept, far_sent = project(tuple(range(far, dp_size)))
    far_came = from_member(far_sent, 1)
    attended = pl.pallas_call(
        join_kernel,
        out_shape=jax.ShapeDtypeStruct((rows, width * dp_size), jnp.bfloat16),
        in_specs=[whole_vmem()] * 4,
        out_specs=whole_vmem(),
        compiler_params=pltpu.CompilerParams(vmem_limit_bytes=vmem_bytes),
    )(near_kept, near_came, far_kept, far_came)
    return (attended, fresh[None])


def solution(mesh):
    in_specs = (
        P(("dp", "tensor"), None),
        P(),
        P("dp", None),
        P(None, "dp", None),
        P(),
        P(),
        P(None, "dp"),
        P(("dp", "tensor"), None, None),
        P("dp"),
        P("dp"),
        P("dp"),
    )
    out_specs = (P(("dp", "tensor"), None), P(("dp", "tensor"), None, None))
    return jax.shard_map(body, mesh=mesh, in_specs=in_specs, out_specs=out_specs, check_vma=False)
```

```python
import functools

import jax
import jax.numpy as jnp
import numpy as np
from jax import lax
from jax.experimental import pallas as pl
from jax.experimental.pallas import tpu as pltpu
from jax.sharding import PartitionSpec as P

epsilon = 1e-05
theta_base = 1000000.0
masked_score = -1e30
column_chunks = 4
vmem_bytes = 32 * 1024 * 1024
most_vmem_bytes = 62 * 1024 * 1024


def lanes_of(value):
    return lax.broadcasted_iota(jnp.int32, value.shape, value.ndim - 1)


def norm_rope(head, gain, cosine, sine):
    mean_square = jnp.mean(head * head, axis=0, keepdims=True)
    normed = head * lax.rsqrt(mean_square + epsilon) * gain
    half_dim = head.shape[0] // 2
    first, second = normed[:half_dim], normed[half_dim:]
    return jnp.concatenate(
        [first * cosine - second * sine, second * cosine + first * sine], axis=0
    )


def table_entry(table, index):
    found = jnp.int32(table[0])
    for place in range(1, len(table)):
        found = jnp.where(index == place, jnp.int32(table[place]), found)
    return found


def stage_kernel(plan, final, *refs):
    old, offsets, parts = plan["old"], plan["offsets"], plan["parts"]
    pieces, head_dim, ring = plan["pieces"], plan["head_dim"], plan["ring"]
    members = len(ring)
    refs = list(refs)

    def take(count):
        taken = refs[:count]
        del refs[:count]
        return taken

    limits_ref = take(1)[0]
    tokens = take(sum(parts))
    norm_gain, head_ref, cache_ref, values_ref = take(4)
    weights = take(pieces)
    if old:
        queries_in, keyval_in, stats_in = take(3)
    if final:
        heads_out = take(members // 2)
        fresh_out = take(1)[0]
    else:
        queries_out, keyval_out, stats_out = take(3)
    normed_ref, projected_ref = take(2)
    if final:
        queries_out, keyval_out, stats_out, joined_ref = take(4)

    fresh_blocks = len(parts)
    blocks = old + fresh_blocks
    rows = normed_ref.shape[0] // fresh_blocks
    lanes = 2 * head_dim
    query_cols = projected_ref.shape[1] - lanes
    heads = query_cols // head_dim
    count = heads * rows
    rank = lax.axis_index("tensor")
    own = lax.axis_index("dp")
    length = limits_ref[0:1, 0:1]
    window_len = limits_ref[1:2, 0:1]
    sink_total = limits_ref[2:3, 0:1]
    place = table_entry([ring.index(one) for one in range(members)], rank % members)
    ids = [table_entry(ring, (place + offset + members) % members) for offset in offsets]

    gain = norm_gain[...]
    start = 0
    for part in tokens:
        values = part[...].astype(jnp.float32)
        mean_square = jnp.mean(values * values, axis=1, keepdims=True)
        normed_ref[pl.ds(start, part.shape[0]), :] = (
            values * lax.rsqrt(mean_square + epsilon) * gain
        ).astype(jnp.bfloat16)
        start += part.shape[0]
    depth = weights[0].shape[0]
    total = None
    for piece in range(pieces):
        from_column = pl.multiple_of((own ^ piece) * depth, depth)
        term = jnp.dot(
            normed_ref[:, pl.ds(from_column, depth)],
            weights[piece][...],
            preferred_element_type=jnp.float32,
        )
        total = term if total is None else total + term
    projected_ref[...] = total
    scale = head_dim ** (-0.5)

    if old and not final:
        queries_out[:, pl.ds(0, old * count)] = queries_in[...]
    if old:
        keyval_out[pl.ds(0, old * rows), :] = keyval_in[...]
    padding = jnp.zeros((head_dim, count), jnp.bfloat16)
    query_gains = head_ref[:head_dim, :]
    key_gains = head_ref[head_dim : 2 * head_dim, :]
    for block in range(fresh_blocks):
        position = length + ids[old + block] * rows + lax.broadcasted_iota(jnp.int32, (1, rows), 1)
        angles = position.astype(jnp.float32) * head_ref[2 * head_dim :, :]
        cosine, sine = jnp.cos(angles), jnp.sin(angles)
        here = pl.ds(block * rows, rows)
        turned = projected_ref[here, :].T
        roped = [
            norm_rope(
                turned[head * head_dim : (head + 1) * head_dim],
                query_gains if head < heads else key_gains,
                cosine,
                sine,
            )
            for head in range(heads + 1)
        ]
        queries = jnp.concatenate(roped[:heads], axis=1).astype(jnp.bfloat16)
        queries = (queries.astype(jnp.float32) * scale).astype(jnp.bfloat16)
        queries_out[:, pl.ds((old + block) * count, count)] = jnp.concatenate(
            [queries, padding], axis=0
        )
        keys = jnp.concatenate([roped[heads], roped[heads]], axis=0).T
        last = projected_ref[here, pl.ds(query_cols, lanes)]
        keyval_out[pl.ds((old + block) * rows, rows), :] = jnp.where(
            lanes_of(last) < head_dim, keys, last
        ).astype(jnp.bfloat16)

    turned = keyval_out[...].astype(jnp.float32).T
    new_values = jnp.where(
        lax.broadcasted_iota(jnp.int32, turned.shape, 0) < head_dim, 1.0, turned
    ).astype(jnp.bfloat16)

    def token_rows(low_block, high_block):
        step = lax.broadcasted_iota(jnp.int32, (rows, 1), 0)
        return jnp.concatenate(
            [step + ids[block] * rows for block in range(low_block, high_block)], axis=0
        )

    lane_token = lax.broadcasted_iota(jnp.int32, (1, count), 1) % rows

    def pack(row_max, sums):
        return jnp.concatenate(
            [
                jnp.broadcast_to(row_max, (8, row_max.shape[1])),
                sums[:8],
                sums[head_dim:],
            ],
            axis=0,
        )

    cache_slots = cache_ref.shape[0]
    key_token = token_rows(0, blocks)

    def attend_new():
        span = pl.ds(old * count, fresh_blocks * count)
        queries = queries_out[:, span]
        at = jnp.concatenate(
            [ids[block] * rows + lane_token for block in range(old, blocks)], axis=1
        )
        scores = jnp.dot(cache_ref[...], queries, preferred_element_type=jnp.float32)
        cached = lax.broadcasted_iota(jnp.int32, (cache_slots, 1), 0)
        far_away = jnp.int32(1 << 29)
        reach = jnp.where(
            cached < length, jnp.where(cached < sink_total, far_away, cached), -far_away
        )
        masked = jnp.where(reach > length - window_len + at, scores, masked_score)
        near_scores = jnp.dot(keyval_out[...], queries, preferred_element_type=jnp.float32)
        near_masked = jnp.where(key_token <= at, near_scores, masked_score)
        row_max = jnp.maximum(
            jnp.max(masked, axis=0, keepdims=True),
            jnp.max(near_masked, axis=0, keepdims=True),
        )
        unnormed = jnp.exp(masked - row_max).astype(jnp.bfloat16)
        near_unnormed = jnp.exp(near_masked - row_max).astype(jnp.bfloat16)
        sums = jnp.dot(
            values_ref[...], unnormed, preferred_element_type=jnp.float32
        ) + jnp.dot(new_values, near_unnormed, preferred_element_type=jnp.float32)
        stats_out[:, span] = pack(row_max, sums)

    if old:
        span = pl.ds(0, old * count)
        at = jnp.concatenate([lane_token + ids[block] * rows for block in range(old)], axis=1)
        near_scores = jnp.dot(
            keyval_out[pl.ds(old * rows, fresh_blocks * rows), :],
            queries_in[...],
            preferred_element_type=jnp.float32,
        )
        near_masked = jnp.where(token_rows(old, blocks) <= at, near_scores, masked_score)
        old_max = stats_in[0:1, :]
        row_max = jnp.maximum(jnp.max(near_masked, axis=0, keepdims=True), old_max)
        unnormed = jnp.exp(near_masked - row_max).astype(jnp.bfloat16)
        sums = jnp.dot(
            new_values[:, old * rows :], unnormed, preferred_element_type=jnp.float32
        )
        before = stats_in[...] * jnp.exp(old_max - row_max)
        stats_out[:, span] = pack(row_max, sums) + jnp.where(
            lax.broadcasted_iota(jnp.int32, before.shape, 0) < 8, 0.0, before
        )

    attend_new()

    if final:
        for block in range(blocks):
            target = pl.ds(pl.multiple_of(ids[block] * rows, rows), rows)
            fresh_out[target, :] = keyval_out[pl.ds(block * rows, rows), :]
            sums = stats_out[:, pl.ds(block * count, count)]
            result = sums[16:] * (1.0 / sums[8:9])
            pair = (ids[block] // 2) ^ (rank % members // 2)
            to_row = pl.multiple_of((pair * 2 + ids[block] % 2) * rows, rows)
            joined_ref[pl.ds(to_row, rows), :] = jnp.concatenate(
                [result[:, head * rows : (head + 1) * rows] for head in range(heads)], axis=0
            ).T.astype(jnp.bfloat16)
        for pair in range(members // 2):
            heads_out[pair][...] = joined_ref[pl.ds(pair * 2 * rows, 2 * rows), :]


def output_kernel(members, held, *refs):
    parts = refs[: members // 2]
    weights = refs[members // 2 : members // 2 + len(held)]
    kept_ref, sent_ref, total_ref = refs[members // 2 + len(held) :]
    rows, depth = kept_ref.shape[0], parts[0].shape[1]
    width = weights[0].shape[1]
    member = lax.axis_index("tensor") % members
    own = lax.axis_index("dp")
    for place, piece in enumerate(held):
        total = None
        for pair in range(members // 2):
            from_row = pl.multiple_of(((member // 2) ^ pair) * depth, depth)
            term = jnp.dot(
                parts[pair][...],
                weights[place][pl.ds(from_row, depth), :],
                preferred_element_type=jnp.float32,
            )
            total = term if total is None else total + term
        total_ref[...] = total
        columns = pl.ds(pl.multiple_of((own ^ piece) % len(held) * width, width), width)
        mine = pl.multiple_of(member % 2 * rows, rows)
        kept_ref[:, columns] = total_ref[pl.ds(mine, rows), :]
        sent_ref[:, columns] = total_ref[pl.ds(rows - mine, rows), :].astype(sent_ref.dtype)


def columns_kernel(members, query_ref, keyval_ref, combined_ref, sides_ref, sems):
    member = lax.axis_index("tensor") % members
    query_cols = query_ref.shape[1] // members
    lanes = combined_ref.shape[1] - query_cols
    from_column = pl.multiple_of(member * query_cols, query_cols)
    pair_column = pl.multiple_of(member // 2 * lanes, lanes)
    depth = query_ref.shape[0]
    chunk = depth // column_chunks
    query_copies, side_copies = [], []
    for part in range(column_chunks):
        some = pl.ds(part * chunk, chunk)
        for side in range(2):
            side_copies.append(
                pltpu.make_async_copy(
                    keyval_ref.at[side, some, pl.ds(pair_column, lanes)],
                    sides_ref.at[side, some],
                    sems.at[side, part],
                )
            )
        query_copies.append(
            pltpu.make_async_copy(
                query_ref.at[some, pl.ds(from_column, query_cols)],
                combined_ref.at[some, pl.ds(0, query_cols)],
                sems.at[2, part],
            )
        )
    copies = side_copies + query_copies
    for copy in copies:
        copy.start()
    for copy in side_copies:
        copy.wait()
    keys, values = sides_ref[0], sides_ref[1]
    head_dim = lanes // 2
    even = member % 2 == 0
    low = lanes_of(keys) < head_dim

    def turned(side):
        return pltpu.roll(side.astype(jnp.float32), head_dim, 1).astype(jnp.bfloat16)

    @pl.when(even)
    def _():
        combined_ref[:, query_cols:] = jnp.where(low, keys, turned(values))

    @pl.when(jnp.logical_not(even))
    def _():
        combined_ref[:, query_cols:] = jnp.where(low, turned(keys), values)

    for copy in query_copies:
        copy.wait()


def join_kernel(place, kept, came, *refs):
    attended_ref, total_ref, sem = refs[-3:]
    width = kept.shape[1]
    side = lax.axis_index("dp") // (lax.axis_size("dp") // 2)
    start = pl.multiple_of((side ^ place) * width, width)
    total_ref[...] = (kept[...] + came[...].astype(jnp.float32)).astype(total_ref.dtype)
    copy = pltpu.make_async_copy(total_ref, attended_ref.at[:, pl.ds(start, width)], sem)
    copy.start()
    copy.wait()


def turn_kernel(members, length_ref, window_ref, sink_ref, *refs):
    cache_ref, norm_gain, query_gain, key_gain, freq_ref = refs[:5]
    values_ref, gain_ref, head_ref, limits_ref = refs[7:]
    turned = cache_ref[0].astype(jnp.float32).T
    row = lax.broadcasted_iota(jnp.int32, turned.shape, 0)
    head_dim = turned.shape[0] // 2
    values_ref[...] = jnp.where(row < head_dim, 1.0, turned).astype(jnp.bfloat16)
    gain = norm_gain[...].astype(jnp.float32)
    gain_ref[...] = jnp.concatenate([gain[one : one + 1] for one in range(gain.shape[0])], axis=1)
    rows = head_ref.shape[1]
    for place, one in enumerate((query_gain, key_gain)):
        head_ref[pl.ds(place * head_dim, head_dim), :] = jnp.broadcast_to(
            one[...], (rows, head_dim)
        ).T
    head_ref[pl.ds(2 * head_dim, head_dim // 2), :] = freq_ref[...]
    slot = lax.axis_index("tensor") // members if length_ref.shape[0] > 1 else 0
    line = lax.broadcasted_iota(jnp.int32, limits_ref.shape, 0)
    limits_ref[...] = jnp.where(
        line == 0, length_ref[slot], jnp.where(line == 1, window_ref[slot], sink_ref[slot])
    )


def whole_vmem():
    return pl.BlockSpec(memory_space=pltpu.VMEM)


def run_stage(plan, final, limits, tokens, shared, weights, state):
    rows = plan["rows"]
    head_dim = plan["head_dim"]
    old, fresh_blocks = plan["old"], len(plan["parts"])
    blocks = old + fresh_blocks
    lanes = 2 * head_dim
    width = weights[0].shape[1]
    query_cols = width - lanes
    count = rows * query_cols // head_dim
    features = tokens[0].shape[1]
    slots = shared[-1].shape[1]
    state_shapes = [
        ((lanes, blocks * count), jnp.bfloat16),
        ((blocks * rows, lanes), jnp.bfloat16),
        ((head_dim + 16, blocks * count), jnp.float32),
    ]
    scratch = [
        pltpu.VMEM((fresh_blocks * rows, features), jnp.bfloat16),
        pltpu.VMEM((fresh_blocks * rows, width), jnp.float32),
    ]
    if final:
        out_shape = (
            *[jax.ShapeDtypeStruct((2 * rows, query_cols), jnp.bfloat16)] * (blocks // 2),
            jax.ShapeDtypeStruct((blocks * rows, lanes), jnp.bfloat16),
        )
        scratch += [pltpu.VMEM(*one) for one in state_shapes]
        scratch += [pltpu.VMEM((blocks * rows, query_cols), jnp.bfloat16)]
    else:
        out_shape = tuple(jax.ShapeDtypeStruct(*one) for one in state_shapes)
    operands = [limits, *tokens, *shared, *weights, *state]
    return pl.pallas_call(
        functools.partial(stage_kernel, plan, final),
        out_shape=out_shape,
        in_specs=[whole_vmem()] * len(operands),
        out_specs=(whole_vmem(),) * len(out_shape),
        scratch_shapes=scratch,
        compiler_params=pltpu.CompilerParams(vmem_limit_bytes=vmem_bytes),
        cost_estimate=pl.CostEstimate(flops=1024, bytes_accessed=1024, transcendentals=0),
    )(*operands)


def body(
    tokens,
    norm_gain,
    query_weight,
    keyval_weight,
    query_gain,
    key_gain,
    output_weight,
    keyval_cache,
    cached_lengths,
    sink_count,
    window,
):
    tensor_rank = lax.axis_index("tensor")
    tensor_size = lax.axis_size("tensor")
    dp_size = lax.axis_size("dp")
    head_dim = query_gain.shape[0]
    kv_heads = keyval_weight.shape[2] // head_dim
    member = tensor_rank % kv_heads
    block_cols = query_weight.shape[1] // kv_heads
    rows = tokens.shape[0]

    if tensor_size == kv_heads == 8:
        ring = [0, 2, 4, 6, 7, 5, 3, 1]
    else:
        ring = list(range(kv_heads))
    def ring_route(step):
        route = []
        for group in range(0, tensor_size, kv_heads):
            for place in range(kv_heads):
                route.append(
                    (group + ring[place], group + ring[(place + step) % kv_heads])
                )
        return route

    def forward(block):
        return lax.ppermute(block, "tensor", ring_route(1))

    def backward(block):
        return lax.ppermute(block, "tensor", ring_route(-1))

    def from_dp(block, apart):
        return lax.ppermute(block, "dp", [(one, one ^ apart) for one in range(dp_size)])

    depth = query_weight.shape[0]
    combined = pl.pallas_call(
        functools.partial(columns_kernel, kv_heads),
        out_shape=jax.ShapeDtypeStruct((depth, block_cols + 2 * head_dim), jnp.bfloat16),
        in_specs=[pl.BlockSpec(memory_space=pltpu.HBM)] * 2,
        out_specs=whole_vmem(),
        scratch_shapes=[
            pltpu.VMEM((2, depth, 2 * head_dim), jnp.bfloat16),
            pltpu.SemaphoreType.DMA((3, column_chunks)),
        ],
        cost_estimate=pl.CostEstimate(flops=0, bytes_accessed=1 << 25, transcendentals=0),
        compiler_params=pltpu.CompilerParams(vmem_limit_bytes=most_vmem_bytes),
    )(query_weight, keyval_weight)
    far = dp_size // 2

    def after(value, *others):
        return lax.optimization_barrier((value, *others))[0]

    pieces = {0: combined, far: from_dp(combined, far)}
    steps = (kv_heads - 1) // 2
    early = min(2, steps)
    chain, chain_offsets = [tokens], [0]
    ahead, behind = tokens, tokens
    for step in range(1, early + 1):
        ahead, behind = forward(ahead), backward(behind)
        chain += [ahead, behind]
        chain_offsets += [-step, step]
    exponents = -2.0 * np.arange(head_dim // 2, dtype=np.float32) / np.float32(head_dim)
    inverse_freq = np.power(np.float32(theta_base), exponents, dtype=np.float32)
    inverse_freq = np.tile(inverse_freq[:, None], (1, rows))
    cache_rows = keyval_cache[0]
    features = norm_gain.shape[0]
    values, gain_row, head_table, limits = pl.pallas_call(
        functools.partial(turn_kernel, kv_heads),
        out_shape=(
            jax.ShapeDtypeStruct(cache_rows.shape[::-1], jnp.bfloat16),
            jax.ShapeDtypeStruct((1, features), jnp.float32),
            jax.ShapeDtypeStruct((2 * head_dim + head_dim // 2, rows), jnp.float32),
            jax.ShapeDtypeStruct((8, 128), jnp.int32),
        ),
        in_specs=[pl.BlockSpec(memory_space=pltpu.SMEM)] * 3
        + [whole_vmem()] * 5
        + [pl.BlockSpec(memory_space=pl.ANY)] * 2,
        out_specs=(whole_vmem(),) * 4,
        compiler_params=pltpu.CompilerParams(vmem_limit_bytes=vmem_bytes),
    )(
        cached_lengths,
        window,
        sink_count,
        keyval_cache,
        norm_gain.reshape(-1, 128),
        query_gain[None],
        key_gain[None],
        jnp.asarray(inverse_freq),
        *chain[1:3],
    )
    out_local = after(output_weight, *chain[1:3]).reshape(kv_heads // 2, 2, block_cols, -1)
    out_local = lax.dynamic_index_in_dim(out_local, member % 2, 1, keepdims=False)
    out_local = out_local.reshape(kv_heads // 2 * block_cols, -1)
    far_out = from_dp(after(out_local, pieces[far], values, *chain[1:]), far)
    pieces[far], values, *unused = lax.optimization_barrier((pieces[far], values, *chain[1:]))
    apart = far // 2
    while apart >= 1:
        for known in list(pieces):
            pieces[known ^ apart] = from_dp(pieces[known], apart)
        apart //= 2
    weights = [pieces[k] for k in range(dp_size)]
    shared = (
        gain_row,
        head_table,
        cache_rows,
        values,
    )

    offsets = []
    state = ()
    arrived, arrived_offsets = chain, chain_offsets
    for step in range(early + 1, steps + 3):
        final = step > steps + 1
        offsets += arrived_offsets
        plan = {
            "old": len(offsets) - len(arrived_offsets),
            "offsets": tuple(offsets),
            "parts": (2,) if final else (1,) * len(arrived),
            "pieces": dp_size,
            "head_dim": head_dim,
            "ring": tuple(ring),
            "rows": rows,
        }
        before = state
        if not final:
            if before:
                ahead, behind = after(ahead, *before), after(behind, *before)
            if step > steps:
                ahead, behind = ahead[: rows // 2], behind[rows // 2 :]
            ahead, behind = forward(ahead), backward(behind)
        state = run_stage(plan, final, limits, arrived, shared, weights, state)
        arrived = [ahead, behind]
        arrived_offsets = [-step, step] if step <= steps else [step]
        if not before:
            out_pieces = {0: after(out_local, *state)}
    *head_out, fresh = state
    def from_member(block, apart):
        route = [(one, one ^ apart) for one in range(tensor_size)]
        return lax.ppermute(block, "tensor", route)

    parts = [head_out[0]] + [
        from_member(head_out[pair], 2 * pair) for pair in range(1, kv_heads // 2)
    ]
    width = output_weight.shape[1]

    def project(held):
        return pl.pallas_call(
            functools.partial(output_kernel, kv_heads, held),
            out_shape=(
                jax.ShapeDtypeStruct((rows, width * len(held)), jnp.float32),
                jax.ShapeDtypeStruct((rows, width * len(held)), jnp.bfloat16),
            ),
            in_specs=[whole_vmem()] * (len(parts) + len(held)),
            out_specs=(whole_vmem(),) * 2,
            scratch_shapes=[pltpu.VMEM((2 * rows, width), jnp.float32)],
            compiler_params=pltpu.CompilerParams(vmem_limit_bytes=vmem_bytes),
        )(*parts, *[out_pieces[piece] for piece in held])

    def spread(known_pieces, apart):
        while apart >= 1:
            for known in known_pieces:
                out_pieces[known ^ apart] = from_dp(out_pieces[known], apart)
            known_pieces = known_pieces + [known ^ apart for known in known_pieces]
            apart //= 2

    spread([0], far // 2)
    near_kept, near_sent = project(tuple(range(far)))
    near_came = from_member(near_sent, 1)
    out_pieces[far] = after(far_out, *parts[1:])
    spread([far], far // 2)
    far_kept, far_sent = project(tuple(range(far, dp_size)))
    far_came = from_member(far_sent, 1)

    def join(place, kept, came, *held):
        return pl.pallas_call(
            functools.partial(join_kernel, place),
            out_shape=jax.ShapeDtypeStruct((rows, width * dp_size), jnp.bfloat16),
            in_specs=[whole_vmem()] * 2 + [pl.BlockSpec(memory_space=pl.ANY)] * len(held),
            out_specs=pl.BlockSpec(memory_space=pl.ANY),
            input_output_aliases={2: 0} if held else {},
            scratch_shapes=[
                pltpu.VMEM(kept.shape, jnp.bfloat16),
                pltpu.SemaphoreType.DMA,
            ],
            compiler_params=pltpu.CompilerParams(vmem_limit_bytes=vmem_bytes),
        )(kept, came, *held)

    attended = join(1, far_kept, far_came, join(0, near_kept, near_came))
    return (attended, fresh[None])


def solution(mesh):
    in_specs = (
        P(("dp", "tensor"), None),
        P(),
        P("dp", None),
        P(None, "dp", None),
        P(),
        P(),
        P(None, "dp"),
        P(("dp", "tensor"), None, None),
        P("dp"),
        P("dp"),
        P("dp"),
    )
    out_specs = (P(("dp", "tensor"), None), P(("dp", "tensor"), None, None))
    return jax.shard_map(body, mesh=mesh, in_specs=in_specs, out_specs=out_specs, check_vma=False)
```

```python
import functools

import jax
import jax.numpy as jnp
import numpy as np
from jax import lax
from jax.experimental import pallas as pl
from jax.experimental.pallas import tpu as pltpu
from jax.sharding import PartitionSpec as P

epsilon = 1e-05
theta_base = 1000000.0
masked_score = -1e30
column_chunks = 4
vmem_bytes = 32 * 1024 * 1024
most_vmem_bytes = 62 * 1024 * 1024


def lanes_of(value):
    return lax.broadcasted_iota(jnp.int32, value.shape, value.ndim - 1)


def norm_rope(head, gain, cosine, sine):
    mean_square = jnp.mean(head * head, axis=0, keepdims=True)
    normed = head * lax.rsqrt(mean_square + epsilon) * gain
    half_dim = head.shape[0] // 2
    first, second = normed[:half_dim], normed[half_dim:]
    return jnp.concatenate(
        [first * cosine - second * sine, second * cosine + first * sine], axis=0
    )


def table_entry(table, index):
    found = jnp.int32(table[0])
    for place in range(1, len(table)):
        found = jnp.where(index == place, jnp.int32(table[place]), found)
    return found


def stage_kernel(plan, final, *refs):
    old, offsets, parts = plan["old"], plan["offsets"], plan["parts"]
    pieces, head_dim, ring = plan["pieces"], plan["head_dim"], plan["ring"]
    members = len(ring)
    refs = list(refs)

    def take(count):
        taken = refs[:count]
        del refs[:count]
        return taken

    limits_ref = take(1)[0]
    tokens = take(sum(parts))
    norm_gain, head_ref, cache_ref, values_ref = take(4)
    weights = take(pieces)
    if old:
        queries_in, keyval_in, stats_in = take(3)
    if final:
        heads_out = take(members // 2)
        fresh_out = take(1)[0]
    else:
        queries_out, keyval_out, stats_out = take(3)
    normed_ref, projected_ref = take(2)
    if final:
        queries_out, keyval_out, stats_out, joined_ref = take(4)

    fresh_blocks = len(parts)
    blocks = old + fresh_blocks
    rows = normed_ref.shape[0] // fresh_blocks
    lanes = 2 * head_dim
    query_cols = projected_ref.shape[1] - lanes
    heads = query_cols // head_dim
    count = heads * rows
    rank = lax.axis_index("tensor")
    own = lax.axis_index("dp")
    length = limits_ref[0:1, 0:1]
    window_len = limits_ref[1:2, 0:1]
    sink_total = limits_ref[2:3, 0:1]
    place = table_entry([ring.index(one) for one in range(members)], rank % members)
    ids = [table_entry(ring, (place + offset + members) % members) for offset in offsets]

    gain = norm_gain[...]
    start = 0
    for part in tokens:
        values = part[...].astype(jnp.float32)
        mean_square = jnp.mean(values * values, axis=1, keepdims=True)
        normed_ref[pl.ds(start, part.shape[0]), :] = (
            values * lax.rsqrt(mean_square + epsilon) * gain
        ).astype(jnp.bfloat16)
        start += part.shape[0]
    depth = weights[0].shape[0]
    total = None
    for piece in range(pieces):
        from_column = pl.multiple_of((own ^ piece) * depth, depth)
        term = jnp.dot(
            normed_ref[:, pl.ds(from_column, depth)],
            weights[piece][...],
            preferred_element_type=jnp.float32,
        )
        total = term if total is None else total + term
    projected_ref[...] = total
    scale = head_dim ** (-0.5)

    if old and not final:
        queries_out[:, pl.ds(0, old * count)] = queries_in[...]
    if old:
        keyval_out[pl.ds(0, old * rows), :] = keyval_in[...]
    padding = jnp.zeros((head_dim, count), jnp.bfloat16)
    query_gains = head_ref[:head_dim, :]
    key_gains = head_ref[head_dim : 2 * head_dim, :]
    for block in range(fresh_blocks):
        position = length + ids[old + block] * rows + lax.broadcasted_iota(jnp.int32, (1, rows), 1)
        angles = position.astype(jnp.float32) * head_ref[2 * head_dim :, :]
        cosine, sine = jnp.cos(angles), jnp.sin(angles)
        here = pl.ds(block * rows, rows)
        turned = projected_ref[here, :].T
        roped = [
            norm_rope(
                turned[head * head_dim : (head + 1) * head_dim],
                query_gains if head < heads else key_gains,
                cosine,
                sine,
            )
            for head in range(heads + 1)
        ]
        queries = jnp.concatenate(roped[:heads], axis=1).astype(jnp.bfloat16)
        queries = (queries.astype(jnp.float32) * scale).astype(jnp.bfloat16)
        queries_out[:, pl.ds((old + block) * count, count)] = jnp.concatenate(
            [queries, padding], axis=0
        )
        keys = jnp.concatenate([roped[heads], roped[heads]], axis=0).T
        last = projected_ref[here, pl.ds(query_cols, lanes)]
        keyval_out[pl.ds((old + block) * rows, rows), :] = jnp.where(
            lanes_of(last) < head_dim, keys, last
        ).astype(jnp.bfloat16)

    turned = keyval_out[...].astype(jnp.float32).T
    new_values = jnp.where(
        lax.broadcasted_iota(jnp.int32, turned.shape, 0) < head_dim, 1.0, turned
    ).astype(jnp.bfloat16)

    def token_rows(low_block, high_block):
        step = lax.broadcasted_iota(jnp.int32, (rows, 1), 0)
        return jnp.concatenate(
            [step + ids[block] * rows for block in range(low_block, high_block)], axis=0
        )

    lane_token = lax.broadcasted_iota(jnp.int32, (1, count), 1) % rows

    def pack(row_max, sums):
        return jnp.concatenate(
            [
                jnp.broadcast_to(row_max, (8, row_max.shape[1])),
                sums[:8],
                sums[head_dim:],
            ],
            axis=0,
        )

    cache_slots = cache_ref.shape[0]
    key_token = token_rows(0, blocks)

    def attend_new():
        span = pl.ds(old * count, fresh_blocks * count)
        queries = queries_out[:, span]
        at = jnp.concatenate(
            [ids[block] * rows + lane_token for block in range(old, blocks)], axis=1
        )
        scores = jnp.dot(cache_ref[...], queries, preferred_element_type=jnp.float32)
        cached = lax.broadcasted_iota(jnp.int32, (cache_slots, 1), 0)
        far_away = jnp.int32(1 << 29)
        reach = jnp.where(
            cached < length, jnp.where(cached < sink_total, far_away, cached), -far_away
        )
        masked = jnp.where(reach > length - window_len + at, scores, masked_score)
        near_scores = jnp.dot(keyval_out[...], queries, preferred_element_type=jnp.float32)
        near_masked = jnp.where(key_token <= at, near_scores, masked_score)
        row_max = jnp.maximum(
            jnp.max(masked, axis=0, keepdims=True),
            jnp.max(near_masked, axis=0, keepdims=True),
        )
        unnormed = jnp.exp(masked - row_max).astype(jnp.bfloat16)
        near_unnormed = jnp.exp(near_masked - row_max).astype(jnp.bfloat16)
        sums = jnp.dot(
            values_ref[...], unnormed, preferred_element_type=jnp.float32
        ) + jnp.dot(new_values, near_unnormed, preferred_element_type=jnp.float32)
        stats_out[:, span] = pack(row_max, sums)

    if old:
        span = pl.ds(0, old * count)
        at = jnp.concatenate([lane_token + ids[block] * rows for block in range(old)], axis=1)
        near_scores = jnp.dot(
            keyval_out[pl.ds(old * rows, fresh_blocks * rows), :],
            queries_in[...],
            preferred_element_type=jnp.float32,
        )
        near_masked = jnp.where(token_rows(old, blocks) <= at, near_scores, masked_score)
        old_max = stats_in[0:1, :]
        row_max = jnp.maximum(jnp.max(near_masked, axis=0, keepdims=True), old_max)
        unnormed = jnp.exp(near_masked - row_max).astype(jnp.bfloat16)
        sums = jnp.dot(
            new_values[:, old * rows :], unnormed, preferred_element_type=jnp.float32
        )
        before = stats_in[...] * jnp.exp(old_max - row_max)
        stats_out[:, span] = pack(row_max, sums) + jnp.where(
            lax.broadcasted_iota(jnp.int32, before.shape, 0) < 8, 0.0, before
        )

    attend_new()

    if final:
        for block in range(blocks):
            target = pl.ds(pl.multiple_of(ids[block] * rows, rows), rows)
            fresh_out[target, :] = keyval_out[pl.ds(block * rows, rows), :]
            sums = stats_out[:, pl.ds(block * count, count)]
            result = sums[16:] * (1.0 / sums[8:9])
            pair = (ids[block] // 2) ^ (rank % members // 2)
            to_row = pl.multiple_of((pair * 2 + ids[block] % 2) * rows, rows)
            joined_ref[pl.ds(to_row, rows), :] = jnp.concatenate(
                [result[:, head * rows : (head + 1) * rows] for head in range(heads)], axis=0
            ).T.astype(jnp.bfloat16)
        for pair in range(members // 2):
            heads_out[pair][...] = joined_ref[pl.ds(pair * 2 * rows, 2 * rows), :]


def output_kernel(members, held, *refs):
    parts = refs[: members // 2]
    weights = refs[members // 2 : members // 2 + len(held)]
    kept_ref, sent_ref, total_ref = refs[members // 2 + len(held) :]
    rows, depth = kept_ref.shape[0], parts[0].shape[1]
    width = weights[0].shape[1]
    member = lax.axis_index("tensor") % members
    own = lax.axis_index("dp")
    for place, piece in enumerate(held):
        total = None
        for pair in range(members // 2):
            from_row = pl.multiple_of(((member // 2) ^ pair) * depth, depth)
            term = jnp.dot(
                parts[pair][...],
                weights[place][pl.ds(from_row, depth), :],
                preferred_element_type=jnp.float32,
            )
            total = term if total is None else total + term
        total_ref[...] = total
        columns = pl.ds(pl.multiple_of((own ^ piece) % len(held) * width, width), width)
        mine = pl.multiple_of(member % 2 * rows, rows)
        kept_ref[:, columns] = total_ref[pl.ds(mine, rows), :]
        sent_ref[:, columns] = total_ref[pl.ds(rows - mine, rows), :].astype(sent_ref.dtype)


def columns_kernel(members, query_ref, keyval_ref, combined_ref, sides_ref, sems):
    member = lax.axis_index("tensor") % members
    query_cols = query_ref.shape[1] // members
    lanes = combined_ref.shape[1] - query_cols
    from_column = pl.multiple_of(member * query_cols, query_cols)
    pair_column = pl.multiple_of(member // 2 * lanes, lanes)
    depth = query_ref.shape[0]
    chunk = depth // column_chunks
    query_copies, side_copies = [], []
    for part in range(column_chunks):
        some = pl.ds(part * chunk, chunk)
        for side in range(2):
            side_copies.append(
                pltpu.make_async_copy(
                    keyval_ref.at[side, some, pl.ds(pair_column, lanes)],
                    sides_ref.at[side, some],
                    sems.at[side, part],
                )
            )
        query_copies.append(
            pltpu.make_async_copy(
                query_ref.at[some, pl.ds(from_column, query_cols)],
                combined_ref.at[some, pl.ds(0, query_cols)],
                sems.at[2, part],
            )
        )
    copies = side_copies + query_copies
    for copy in copies:
        copy.start()
    for copy in side_copies:
        copy.wait()
    keys, values = sides_ref[0], sides_ref[1]
    head_dim = lanes // 2
    even = member % 2 == 0
    low = lanes_of(keys) < head_dim

    def turned(side):
        return pltpu.roll(side.astype(jnp.float32), head_dim, 1).astype(jnp.bfloat16)

    @pl.when(even)
    def _():
        combined_ref[:, query_cols:] = jnp.where(low, keys, turned(values))

    @pl.when(jnp.logical_not(even))
    def _():
        combined_ref[:, query_cols:] = jnp.where(low, turned(keys), values)

    for copy in query_copies:
        copy.wait()


def join_kernel(near_kept, near_came, far_kept, far_came, attended_ref, total_ref, sems):
    width = near_kept.shape[1]
    side = lax.axis_index("dp") // (lax.axis_size("dp") // 2)
    copies = []
    for place, (kept, came) in enumerate(((near_kept, near_came), (far_kept, far_came))):
        start = pl.multiple_of((side ^ place) * width, width)
        total_ref[place] = (kept[...] + came[...].astype(jnp.float32)).astype(total_ref.dtype)
        copies.append(
            pltpu.make_async_copy(
                total_ref.at[place], attended_ref.at[:, pl.ds(start, width)], sems.at[place]
            )
        )
        copies[place].start()
    for copy in copies:
        copy.wait()


def turn_kernel(members, length_ref, window_ref, sink_ref, *refs):
    cache_ref, norm_gain, query_gain, key_gain, freq_ref = refs[:5]
    values_ref, gain_ref, head_ref, limits_ref = refs[7:]
    turned = cache_ref[0].astype(jnp.float32).T
    row = lax.broadcasted_iota(jnp.int32, turned.shape, 0)
    head_dim = turned.shape[0] // 2
    values_ref[...] = jnp.where(row < head_dim, 1.0, turned).astype(jnp.bfloat16)
    gain = norm_gain[...].astype(jnp.float32)
    gain_ref[...] = jnp.concatenate([gain[one : one + 1] for one in range(gain.shape[0])], axis=1)
    rows = head_ref.shape[1]
    for place, one in enumerate((query_gain, key_gain)):
        head_ref[pl.ds(place * head_dim, head_dim), :] = jnp.broadcast_to(
            one[...], (rows, head_dim)
        ).T
    head_ref[pl.ds(2 * head_dim, head_dim // 2), :] = freq_ref[...]
    slot = lax.axis_index("tensor") // members if length_ref.shape[0] > 1 else 0
    line = lax.broadcasted_iota(jnp.int32, limits_ref.shape, 0)
    limits_ref[...] = jnp.where(
        line == 0, length_ref[slot], jnp.where(line == 1, window_ref[slot], sink_ref[slot])
    )


def whole_vmem():
    return pl.BlockSpec(memory_space=pltpu.VMEM)


def run_stage(plan, final, limits, tokens, shared, weights, state):
    rows = plan["rows"]
    head_dim = plan["head_dim"]
    old, fresh_blocks = plan["old"], len(plan["parts"])
    blocks = old + fresh_blocks
    lanes = 2 * head_dim
    width = weights[0].shape[1]
    query_cols = width - lanes
    count = rows * query_cols // head_dim
    features = tokens[0].shape[1]
    slots = shared[-1].shape[1]
    state_shapes = [
        ((lanes, blocks * count), jnp.bfloat16),
        ((blocks * rows, lanes), jnp.bfloat16),
        ((head_dim + 16, blocks * count), jnp.float32),
    ]
    scratch = [
        pltpu.VMEM((fresh_blocks * rows, features), jnp.bfloat16),
        pltpu.VMEM((fresh_blocks * rows, width), jnp.float32),
    ]
    if final:
        out_shape = (
            *[jax.ShapeDtypeStruct((2 * rows, query_cols), jnp.bfloat16)] * (blocks // 2),
            jax.ShapeDtypeStruct((blocks * rows, lanes), jnp.bfloat16),
        )
        scratch += [pltpu.VMEM(*one) for one in state_shapes]
        scratch += [pltpu.VMEM((blocks * rows, query_cols), jnp.bfloat16)]
    else:
        out_shape = tuple(jax.ShapeDtypeStruct(*one) for one in state_shapes)
    operands = [limits, *tokens, *shared, *weights, *state]
    return pl.pallas_call(
        functools.partial(stage_kernel, plan, final),
        out_shape=out_shape,
        in_specs=[whole_vmem()] * len(operands),
        out_specs=(whole_vmem(),) * len(out_shape),
        scratch_shapes=scratch,
        compiler_params=pltpu.CompilerParams(vmem_limit_bytes=vmem_bytes),
        cost_estimate=pl.CostEstimate(flops=1024, bytes_accessed=1024, transcendentals=0),
    )(*operands)


def body(
    tokens,
    norm_gain,
    query_weight,
    keyval_weight,
    query_gain,
    key_gain,
    output_weight,
    keyval_cache,
    cached_lengths,
    sink_count,
    window,
):
    tensor_rank = lax.axis_index("tensor")
    tensor_size = lax.axis_size("tensor")
    dp_size = lax.axis_size("dp")
    head_dim = query_gain.shape[0]
    kv_heads = keyval_weight.shape[2] // head_dim
    member = tensor_rank % kv_heads
    block_cols = query_weight.shape[1] // kv_heads
    rows = tokens.shape[0]

    if tensor_size == kv_heads == 8:
        ring = [0, 2, 4, 6, 7, 5, 3, 1]
    else:
        ring = list(range(kv_heads))
    def ring_route(step):
        route = []
        for group in range(0, tensor_size, kv_heads):
            for place in range(kv_heads):
                route.append(
                    (group + ring[place], group + ring[(place + step) % kv_heads])
                )
        return route

    def forward(block):
        return lax.ppermute(block, "tensor", ring_route(1))

    def backward(block):
        return lax.ppermute(block, "tensor", ring_route(-1))

    def from_dp(block, apart):
        return lax.ppermute(block, "dp", [(one, one ^ apart) for one in range(dp_size)])

    depth = query_weight.shape[0]
    combined = pl.pallas_call(
        functools.partial(columns_kernel, kv_heads),
        out_shape=jax.ShapeDtypeStruct((depth, block_cols + 2 * head_dim), jnp.bfloat16),
        in_specs=[pl.BlockSpec(memory_space=pltpu.HBM)] * 2,
        out_specs=whole_vmem(),
        scratch_shapes=[
            pltpu.VMEM((2, depth, 2 * head_dim), jnp.bfloat16),
            pltpu.SemaphoreType.DMA((3, column_chunks)),
        ],
        cost_estimate=pl.CostEstimate(flops=0, bytes_accessed=1 << 25, transcendentals=0),
        compiler_params=pltpu.CompilerParams(vmem_limit_bytes=most_vmem_bytes),
    )(query_weight, keyval_weight)
    far = dp_size // 2

    def after(value, *others):
        return lax.optimization_barrier((value, *others))[0]

    pieces = {0: combined, far: from_dp(combined, far)}
    steps = (kv_heads - 1) // 2
    early = min(2, steps)
    chain, chain_offsets = [tokens], [0]
    ahead, behind = tokens, tokens
    for step in range(1, early + 1):
        ahead, behind = forward(ahead), backward(behind)
        chain += [ahead, behind]
        chain_offsets += [-step, step]
    exponents = -2.0 * np.arange(head_dim // 2, dtype=np.float32) / np.float32(head_dim)
    inverse_freq = np.power(np.float32(theta_base), exponents, dtype=np.float32)
    inverse_freq = np.tile(inverse_freq[:, None], (1, rows))
    cache_rows = keyval_cache[0]
    features = norm_gain.shape[0]
    values, gain_row, head_table, limits = pl.pallas_call(
        functools.partial(turn_kernel, kv_heads),
        out_shape=(
            jax.ShapeDtypeStruct(cache_rows.shape[::-1], jnp.bfloat16),
            jax.ShapeDtypeStruct((1, features), jnp.float32),
            jax.ShapeDtypeStruct((2 * head_dim + head_dim // 2, rows), jnp.float32),
            jax.ShapeDtypeStruct((8, 128), jnp.int32),
        ),
        in_specs=[pl.BlockSpec(memory_space=pltpu.SMEM)] * 3
        + [whole_vmem()] * 5
        + [pl.BlockSpec(memory_space=pl.ANY)] * 2,
        out_specs=(whole_vmem(),) * 4,
        compiler_params=pltpu.CompilerParams(vmem_limit_bytes=vmem_bytes),
    )(
        cached_lengths,
        window,
        sink_count,
        keyval_cache,
        norm_gain.reshape(-1, 128),
        query_gain[None],
        key_gain[None],
        jnp.asarray(inverse_freq),
        *chain[1:3],
    )
    out_local = after(output_weight, *chain[1:3]).reshape(kv_heads // 2, 2, block_cols, -1)
    out_local = lax.dynamic_index_in_dim(out_local, member % 2, 1, keepdims=False)
    out_local = out_local.reshape(kv_heads // 2 * block_cols, -1)
    far_out = from_dp(after(out_local, pieces[far], values, *chain[1:]), far)
    pieces[far], values, *unused = lax.optimization_barrier((pieces[far], values, *chain[1:]))
    apart = far // 2
    while apart >= 1:
        for known in list(pieces):
            pieces[known ^ apart] = from_dp(pieces[known], apart)
        apart //= 2
    weights = [pieces[k] for k in range(dp_size)]
    shared = (
        gain_row,
        head_table,
        cache_rows,
        values,
    )

    offsets = []
    state = ()
    arrived, arrived_offsets = chain, chain_offsets
    for step in range(early + 1, steps + 3):
        final = step > steps + 1
        offsets += arrived_offsets
        plan = {
            "old": len(offsets) - len(arrived_offsets),
            "offsets": tuple(offsets),
            "parts": (2,) if final else (1,) * len(arrived),
            "pieces": dp_size,
            "head_dim": head_dim,
            "ring": tuple(ring),
            "rows": rows,
        }
        before = state
        if not final:
            if before:
                ahead, behind = after(ahead, *before), after(behind, *before)
            if step > steps:
                ahead, behind = ahead[: rows // 2], behind[rows // 2 :]
            ahead, behind = forward(ahead), backward(behind)
        state = run_stage(plan, final, limits, arrived, shared, weights, state)
        arrived = [ahead, behind]
        arrived_offsets = [-step, step] if step <= steps else [step]
        if not before:
            out_pieces = {0: after(out_local, *state)}
    *head_out, fresh = state
    def from_member(block, apart):
        route = [(one, one ^ apart) for one in range(tensor_size)]
        return lax.ppermute(block, "tensor", route)

    parts = [head_out[0]] + [
        from_member(head_out[pair], 2 * pair) for pair in range(1, kv_heads // 2)
    ]
    width = output_weight.shape[1]

    def project(held):
        return pl.pallas_call(
            functools.partial(output_kernel, kv_heads, held),
            out_shape=(
                jax.ShapeDtypeStruct((rows, width * len(held)), jnp.float32),
                jax.ShapeDtypeStruct((rows, width * len(held)), jnp.bfloat16),
            ),
            in_specs=[whole_vmem()] * (len(parts) + len(held)),
            out_specs=(whole_vmem(),) * 2,
            scratch_shapes=[pltpu.VMEM((2 * rows, width), jnp.float32)],
            compiler_params=pltpu.CompilerParams(vmem_limit_bytes=vmem_bytes),
        )(*parts, *[out_pieces[piece] for piece in held])

    def spread(known_pieces, apart):
        while apart >= 1:
            for known in known_pieces:
                out_pieces[known ^ apart] = from_dp(out_pieces[known], apart)
            known_pieces = known_pieces + [known ^ apart for known in known_pieces]
            apart //= 2

    spread([0], far // 2)
    near_kept, near_sent = project(tuple(range(far)))
    near_came = from_member(near_sent, 1)
    out_pieces[far] = after(far_out, *parts[1:])
    spread([far], far // 2)
    far_kept, far_sent = project(tuple(range(far, dp_size)))
    far_came = from_member(far_sent, 1)
    attended = pl.pallas_call(
        join_kernel,
        out_shape=jax.ShapeDtypeStruct((rows, width * dp_size), jnp.bfloat16),
        in_specs=[whole_vmem()] * 4,
        out_specs=pl.BlockSpec(memory_space=pl.ANY),
        scratch_shapes=[
            pltpu.VMEM((2, *near_kept.shape), jnp.bfloat16),
            pltpu.SemaphoreType.DMA((2,)),
        ],
        compiler_params=pltpu.CompilerParams(vmem_limit_bytes=vmem_bytes),
    )(near_kept, near_came, far_kept, far_came)
    return (attended, fresh[None])


def solution(mesh):
    in_specs = (
        P(("dp", "tensor"), None),
        P(),
        P("dp", None),
        P(None, "dp", None),
        P(),
        P(),
        P(None, "dp"),
        P(("dp", "tensor"), None, None),
        P("dp"),
        P("dp"),
        P("dp"),
    )
    out_specs = (P(("dp", "tensor"), None), P(("dp", "tensor"), None, None))
    return jax.shard_map(body, mesh=mesh, in_specs=in_specs, out_specs=out_specs, check_vma=False)
```
